32 devices in a mesh: dom: 8 (over z, x), hid: 4 (over y, core).
Axes of the slice: x: 2, y: 2, z: 4, core: 2. Of those that a mesh axis runs over, the one named last changes fastest.
Arguments:
- particles: bfloat16 [8, 1026, 4096], P('dom', None, 'hid')
- noise: bfloat16 [8, 1026, 4096], P('dom', None, 'hid'), may hold values from -5 to 5
- ancestors: int32 [8], P('dom'), may hold values from 0 to 7
- accepted: int32 [8], P('dom'), may hold values 0 or 1
- data: bfloat16 [320, 1024], replicated, may hold values from -6 to 6
- targets: float32 [320], replicated, may hold values from -6 to 6
Outputs:
- moved: bfloat16 [8, 1026, 4096], P('dom', None, 'hid')
- fit: float32 [8], P('dom')
The draws below stay inside these ranges and needn't reach their ends.
All inputs are finite; a program needn't handle non-finite values. No bound on the sum of `accepted` on one device may be relied on, other than what follows from the above.
Results may differ from the reference program's by a relative error of at most 0.0036.
Values may be sent and summed in bfloat16 or wider, within the bound.
A program may use at most 128 MiB of HBM per device.

```python
import math
import jax
import jax.numpy as jnp
import numpy as np
from jax import lax

D_IN = 1024
H = 4096
ROWS = 320
LEAPFROG = 2
PARTICLES = 8


def draw_particles(key, part):
    keys = jax.random.split(key, 3)
    shape = (PARTICLES, D_IN + 2, H)
    row_index = jnp.arange(D_IN + 2)[None, :, None]
    row_factor = jnp.where(row_index == D_IN, 0.1, 1.0).astype(jnp.float32)
    spread = jnp.exp(jax.random.uniform(keys[1], (1, D_IN + 2, H), jnp.float32, math.log(0.5), math.log(2.0))) * row_factor
    tilt = jnp.exp(jax.random.uniform(keys[2], (PARTICLES, 1, 1), jnp.float32, math.log(0.6), math.log(1.6)))
    potential_values = jax.random.normal(keys[0], shape, jnp.float32)
    result = spread * tilt * potential_values
    return result.astype(jnp.bfloat16)


def touch_ends(drawn, stream_key, smallest, top_value):
    longest = drawn.shape.index(max(drawn.shape))
    spots = []
    for shift in (0, 1):
        where = [jax.random.randint(jax.random.fold_in(stream_key, axis), (), 0, length) for axis, length in enumerate(drawn.shape)]
        where[longest] = (where[longest] + shift) % drawn.shape[longest]
        spots.append(tuple(where))
    return drawn.at[spots[0]].set(smallest).at[spots[1]].set(top_value)


def shard_levels(key, dims, cuts, least, largest):
    def one(dim, blocks):
        heights = jax.random.uniform(jax.random.fold_in(jax.random.fold_in(key, 6), dim), (blocks,), jnp.float32, least / len(cuts), largest / len(cuts))
        return jnp.repeat(jnp.exp(heights), dims[dim] // blocks).reshape((-1,) + (1,) * (len(dims) - dim - 1))

    factor_of = one(*cuts[0])
    for cut in cuts[1:]:
        factor_of = factor_of * one(*cut)
    return factor_of


def rank_bounds(amount, slope):
    loads = [(1 << 20) // math.isqrt(grade ** slope) + 1 for grade in range(1, amount + 1)]
    scale = 1 + sum(loads) // (1 << 30)
    return np.cumsum(np.array([max(1, weight // scale) for weight in loads]))


def ranked(stream_key, dims, count, skew):
    table = rank_bounds(count, skew)
    ticket = jax.random.randint(jax.random.fold_in(stream_key, 1), dims, 0, int(table[count - 1]))
    rank = jnp.searchsorted(jnp.asarray(table, jnp.int32), ticket, side="right")
    return jax.random.permutation(jax.random.fold_in(stream_key, 2), count)[rank].astype(jnp.int32)


def scatter_about(own_key, extent, deviation, most, cuts=(), dtype=jnp.bfloat16):
    loudness = shard_levels(own_key, extent, cuts, -0.22, 0.18) if cuts else 1.0
    array = jax.random.normal(own_key, extent, jnp.float32) * deviation * loudness
    return jnp.minimum(jnp.maximum(array, -most), most).astype(dtype)


def setup_inputs(seed: int = 0) -> dict:
    key_of = jax.random.split(jax.random.key(seed), 7)
    particles = draw_particles(jax.random.fold_in(key_of[6], 71), 0)
    noise = scatter_about(key_of[1], (PARTICLES, D_IN + 2, H), 1.0, 5.0, ((0, 8), (2, 4)))
    ancestors = touch_ends(ranked(key_of[2], (PARTICLES,), PARTICLES, 2), jax.random.fold_in(key_of[2], 3), 0, PARTICLES - 1).astype(jnp.int32)
    accepted = touch_ends((jax.random.randint(key_of[3], (PARTICLES,), 0, 4) < 3).astype(jnp.int32), jax.random.fold_in(key_of[3], 1), 0, 1)
    data = scatter_about(key_of[4], (ROWS, D_IN), 1.0, 6.0)
    targets = scatter_about(key_of[5], (ROWS,), 1.0, 6.0, (), jnp.float32)
    return {"particles": particles, "noise": noise, "ancestors": ancestors, "accepted": accepted, "data": data, "targets": targets}


TEMPER_LEVEL = 0.125
NOISE_INV_VARIANCE = 4.0
STEP_SIZE = 0.4

def compute_potential(position, data, in_scale, out_scale):
    weights = position[:-2].astype(jnp.bfloat16)
    preact = jnp.dot(data, weights, preferred_element_type=jnp.float32) * in_scale + position[-2][None, :]
    hidden = jnp.tanh(preact)
    network_outputs = jnp.dot(hidden, position[-1], precision=lax.Precision.HIGHEST) * out_scale
    return (hidden, network_outputs)

def potential_gradient(position, hidden, network_outputs, data, targets, in_scale, out_scale):
    fit_residual = TEMPER_LEVEL * NOISE_INV_VARIANCE * (network_outputs - targets)
    out_weight = position[-1]
    grad_out = jnp.dot(fit_residual, hidden, precision=lax.Precision.HIGHEST) * out_scale + out_weight
    backward = fit_residual[:, None] * (out_weight * out_scale)[None, :] * (1.0 - hidden * hidden)
    grad_bias = lax.optimization_barrier(jnp.sum(backward, axis=0)) + position[-2]
    grad_weight = jnp.dot(data.T, backward.astype(jnp.bfloat16), preferred_element_type=jnp.float32) * in_scale + position[:-2]
    return jnp.concatenate([grad_weight, grad_bias[None, :], grad_out[None, :]], axis=0)

def reference(particles, noise, ancestors, accepted, data, targets):
    resampled = jnp.take(particles, ancestors.astype(jnp.int32), axis=0)
    mean_value = lax.optimization_barrier(jnp.sum(resampled.astype(jnp.float32), axis=0)) / PARTICLES
    mean_square = lax.optimization_barrier(jnp.sum(jnp.square(resampled.astype(jnp.float32)), axis=0)) / PARTICLES
    shrink = PARTICLES / (PARTICLES + 5.0)
    floor_term = 0.001 * 5.0 / (PARTICLES + 5.0)
    inv_mass = (shrink * (mean_square - mean_value * mean_value) + floor_term).astype(jnp.bfloat16).astype(jnp.float32)
    in_scale = D_IN ** (-0.5)
    out_scale = H ** (-0.5)

    def move_one(items):
        start, draws, flag = items
        position0 = start.astype(jnp.float32)
        momentum = draws.astype(jnp.float32) / jnp.sqrt(inv_mass)
        hidden, initial_outputs0 = compute_potential(position0, data, in_scale, out_scale)
        grad = potential_gradient(position0, hidden, initial_outputs0, data, targets, in_scale, out_scale)
        position = position0
        network_outputs = initial_outputs0
        for section in range(LEAPFROG):
            momentum = momentum - 0.5 * STEP_SIZE * grad
            position = position + STEP_SIZE * inv_mass * momentum
            hidden, network_outputs = compute_potential(position, data, in_scale, out_scale)
            if section + 1 < LEAPFROG:
                grad = potential_gradient(position, hidden, network_outputs, data, targets, in_scale, out_scale)
                momentum = momentum - 0.5 * STEP_SIZE * grad
        fit_start = jnp.mean(jnp.square(targets - initial_outputs0))
        fit_end = jnp.mean(jnp.square(targets - network_outputs))
        keep = flag == 1
        moved = jnp.where(keep, position, position0).astype(jnp.bfloat16)
        return (moved, jnp.where(keep, fit_end, fit_start))
    moved, fit = lax.map(move_one, (resampled, noise, accepted))
    return (moved, fit)
```

```python
import functools

import jax
import jax.numpy as jnp
from jax import lax
from jax.experimental import pallas as pl
from jax.experimental.pallas import tpu as pltpu
from jax.sharding import PartitionSpec as P

TEMPER_LEVEL = 0.125
NOISE_INV_VARIANCE = 4.0
STEP_SIZE = 0.4
MESH = pl.DeviceIdType.MESH
TILE = 256
CHUNK = 16


def kernel(
    groups, hids,
    anc_ref, acc_ref, tail_ref, part_ref, noise_ref, data_ref, tgt_ref,
    main_out, tail_out, fit_out,
    anc_all, anc_s, tails, recv, picked, theta0, mass, noise_v, mom, pos, moved, hid, resid,
    tpos, tpos0, tmom, tinv, tout, part_buf, part_all,
    anc_ss, anc_rs, tail_ss, tail_rs, p_ss, p_rs, q_ss, q_rs,
    up_ss, down_ss, side_ss, mass_rs, h_ss, h_rs, loc,
):
    me = lax.axis_index("dom")
    my_hid = lax.axis_index("hid")
    depth, width = theta0.shape
    rows = depth // groups
    data_rows = data_ref.shape[0]
    padded = part_buf.shape[-1]
    in_scale = depth ** (-0.5)
    out_scale = (width * hids) ** (-0.5)
    half = groups // 2
    offsets = []
    for s in range(groups - 1):
        offsets.append(half + (s + 1) // 2 * (1 if s % 2 else -1))

    def wrap(i, n):
        return lax.rem(i, n)

    def block(i):
        return pl.ds(pl.multiple_of(i * rows, rows), rows)

    noise_copy = pltpu.make_async_copy(noise_ref.at[0, pl.ds(0, depth)], noise_v, loc.at[0])
    noise_copy.start()
    own_copy = pltpu.make_async_copy(part_ref.at[0, block(me)], recv.at[me], loc.at[1])
    own_copy.start()
    anc_all[me] = anc_ref[...]
    tails[me] = tail_ref[...]

    barrier = pltpu.get_barrier_semaphore()
    for k in range(1, groups):
        pl.semaphore_signal(barrier, inc=1, device_id=(wrap(me + k, groups), my_hid), device_id_type=MESH)
    for k in range(1, hids):
        pl.semaphore_signal(barrier, inc=1, device_id=(me, wrap(my_hid + k, hids)), device_id_type=MESH)
    pl.semaphore_wait(barrier, groups - 1 + hids - 1)

    def anc_copy(t, slot):
        return pltpu.make_async_remote_copy(
            anc_all.at[slot], anc_all.at[slot], anc_ss.at[t], anc_rs.at[slot],
            device_id=(t, my_hid), device_id_type=MESH)

    def tail_copy(t, slot):
        return pltpu.make_async_remote_copy(
            tails.at[slot], tails.at[slot], tail_ss.at[t], tail_rs.at[slot],
            device_id=(t, my_hid), device_id_type=MESH)

    def part_copy(t, slot):
        return pltpu.make_async_remote_copy(
            part_ref.at[0, block(t)], recv.at[slot], p_ss.at[t], p_rs.at[slot],
            device_id=(t, my_hid), device_id_type=MESH)

    def pick_copy(t, slot):
        return pltpu.make_async_remote_copy(
            picked.at[t], theta0.at[block(slot)], q_ss.at[t], q_rs.at[slot],
            device_id=(t, my_hid), device_id_type=MESH)

    for k in offsets:
        t = wrap(me + k, groups)
        anc_copy(t, me).start()
    for k in offsets:
        t = wrap(me + k, groups)
        part_copy(t, me).start()
    for k in offsets:
        t = wrap(me + k, groups)
        tail_copy(t, me).start()

    for k in offsets:
        s = wrap(me + groups - k, groups)
        anc_copy(s, s).wait_recv()
    scalars = pltpu.make_async_copy(anc_all, anc_s, loc.at[2])
    scalars.start()
    scalars.wait()
    own_copy.wait()
    for k in offsets:
        s = wrap(me + groups - k, groups)
        part_copy(s, s).wait_recv()

    shrink = groups / (groups + 5.0)
    floor_term = 0.001 * 5.0 / (groups + 5.0)

    def finish(total, square):
        mean = total / groups
        return (shrink * (square / groups - mean * mean) + floor_term).astype(jnp.bfloat16)

    my_rows = block(me)

    @pl.loop(0, rows // CHUNK)
    def _(r):
        here = pl.ds(pl.multiple_of(r * CHUNK, CHUNK), CHUNK)

        def add(i, carry):
            total, square = carry
            got = recv[anc_s[i, 0, 0], here]
            picked[i, here] = got
            wide = got.astype(jnp.float32)
            return total + wide, square + wide * wide

        zero = jnp.zeros((CHUNK, width), jnp.float32)
        carry = (zero, zero)
        if groups <= 8:
            for i in range(groups):
                carry = add(i, carry)
        else:
            carry = lax.fori_loop(0, groups, add, carry)
        mass[pl.ds(pl.multiple_of(me * rows + r * CHUNK, CHUNK), CHUNK)] = finish(*carry)
        theta0[pl.ds(pl.multiple_of(me * rows + r * CHUNK, CHUNK), CHUNK)] = picked[me, here]

    place, inner = me // 2, lax.rem(me, 2)

    def mass_copy(t, who, sem):
        return pltpu.make_async_remote_copy(
            mass.at[block(who)], mass.at[block(who)], sem.at[who], mass_rs.at[who],
            device_id=(t, my_hid), device_id_type=MESH)

    def spread(who, up, down):
        if up:
            @pl.when(place < half - 1)
            def _():
                mass_copy(me + 2, who, up_ss).start()
        if down:
            @pl.when(place > 0)
            def _():
                mass_copy(me - 2, who, down_ss).start()
        mass_copy(me + 1 - 2 * inner, who, side_ss).start()

    spread(me, True, True)
    for k in offsets:
        pick_copy(wrap(me + k, groups), me).start()

    for k in offsets:
        s = wrap(me + groups - k, groups)
        tail_copy(s, s).wait_recv()

    def add_tail(i, carry):
        total, square = carry
        wide = tails[anc_s[i, 0, 0]].astype(jnp.float32)
        return total + wide, square + wide * wide

    zero = jnp.zeros((16, width), jnp.float32)
    tinv[...] = finish(*lax.fori_loop(0, groups, add_tail, (zero, zero))).astype(jnp.float32)
    tpos0[...] = tails[anc_s[me, 0, 0]].astype(jnp.float32)
    tpos[...] = tpos0[...]
    tmom[0:2] = tail_ref[...].astype(jnp.float32)[2:4] * lax.rsqrt(tinv[0:2])

    for s in range(1, half):
        @pl.when(place >= s)
        def _():
            mass_copy(me, me - 2 * s, up_ss).wait_recv()
            spread(me - 2 * s, True, False)

        @pl.when(place + s < half)
        def _():
            mass_copy(me, me + 2 * s, up_ss).wait_recv()
            spread(me + 2 * s, False, True)

    for k in offsets:
        s = wrap(me + groups - k, groups)
        pick_copy(s, s).wait_recv()

    data = data_ref[...]

    def forward(weights, cols, keep_hidden):
        pre = jnp.dot(data_ref[...], weights, preferred_element_type=jnp.float32)
        h = jnp.tanh(pre * in_scale + tpos[0:1, cols])
        if keep_hidden:
            hid[:, cols] = h
        weighted = h * tpos[1:2, cols]
        total = weighted[:, 0:128]
        for c in range(128, TILE, 128):
            total = total + weighted[:, c:c + 128]
        return total

    def tile(c):
        return pl.ds(pl.multiple_of(c * TILE, TILE), TILE)

    none = jnp.zeros((data_rows, 128), jnp.float32)

    def outputs(stage, total):
        total = jnp.concatenate([total, jnp.zeros((padded - data_rows, 128), jnp.float32)], axis=0)
        flat = jnp.sum(jnp.transpose(total), axis=0, keepdims=True) * out_scale
        part_buf[stage] = jnp.broadcast_to(flat, (8, padded))

        def copy(t, slot):
            return pltpu.make_async_remote_copy(
                part_buf.at[stage], part_all.at[stage, slot], h_ss.at[stage, t], h_rs.at[stage, slot],
                device_id=(me, t), device_id_type=MESH)

        for k in range(1, hids):
            copy(wrap(my_hid + k, hids), my_hid).start()
        part_all[stage, my_hid] = part_buf[stage]
        for k in range(1, hids):
            s = wrap(my_hid + k, hids)
            copy(s, s).wait_recv()
        for k in range(1, hids):
            copy(wrap(my_hid + k, hids), my_hid).wait_send()
        result = part_all[stage, 0]
        for j in range(1, hids):
            result = result + part_all[stage, j]
        return result[0:1]

    def set_resid(result):
        r = TEMPER_LEVEL * NOISE_INV_VARIANCE * (result - tgt_ref[...])
        column = jnp.transpose(jnp.broadcast_to(r, (128, padded)))[0:data_rows]
        for c in range(0, TILE, 128):
            resid[:, c:c + 128] = column

    keep = acc_ref[0] == 1

    def move(first, c, total):
        cols = tile(c)
        h = hid[:, cols]
        b, v = tpos[0:1, cols], tpos[1:2, cols]
        res = resid[...]
        grad_v = jnp.sum(res * h, axis=0, keepdims=True) * out_scale + v
        back = res * (v * out_scale) * (1.0 - h * h)
        grad_b = jnp.sum(back, axis=0, keepdims=True) + b
        grad = lax.dot_general(data_ref[...], back.astype(jnp.bfloat16), (((0,), (0,)), ((), ())),
                               preferred_element_type=jnp.float32) * in_scale
        step = 0.5 * STEP_SIZE if first else STEP_SIZE
        grad_t = jnp.concatenate([grad_b, grad_v], axis=0)
        tm = tmom[0:2, cols] - step * grad_t
        tmom[0:2, cols] = tm
        tpos[0:2, cols] = tpos[0:2, cols] + STEP_SIZE * tinv[0:2, cols] * tm
        inv = mass[:, cols].astype(jnp.float32)
        w0 = theta0[:, cols].astype(jnp.float32)
        if first:
            m = noise_v[:, cols].astype(jnp.float32) * lax.rsqrt(inv) - step * (grad + w0)
            w = w0 + STEP_SIZE * inv * m
            mom[:, cols] = m
            pos[:, cols] = w
        else:
            w = pos[:, cols]
            m = mom[:, cols] - step * (grad + w)
            w = w + STEP_SIZE * inv * m
            moved[:, cols] = jnp.where(keep, w, w0).astype(jnp.bfloat16)
        return total + forward(w.astype(jnp.bfloat16), cols, first)

    start = lax.fori_loop(
        0, width // TILE, lambda c, total: total + forward(theta0[:, tile(c)], tile(c), True), none)
    outputs0 = outputs(0, start)
    set_resid(outputs0)

    noise_copy.wait()
    other = 1 - 2 * inner
    for q in range(half):
        mass_copy(me, 2 * q + 1 - inner, side_ss).wait_recv()

    outputs1 = outputs(1, lax.fori_loop(0, width // TILE, functools.partial(move, True), none))
    set_resid(outputs1)
    last = lax.fori_loop(0, width // TILE, functools.partial(move, False), none)
    result_copy = pltpu.make_async_copy(moved, main_out, loc.at[3])
    result_copy.start()
    outputs2 = outputs(2, last)
    tout[...] = jnp.zeros_like(tout)
    tout[0:2] = jnp.where(keep, tpos[0:2], tpos0[0:2])
    tail_out[...] = tout[...].astype(jnp.bfloat16)
    miss = tgt_ref[...] - jnp.where(keep, outputs2, outputs0)
    fit = jnp.sum(miss * miss, axis=1, keepdims=True) / data_rows
    fit_out[...] = jnp.broadcast_to(fit, fit_out.shape)

    result_copy.wait()
    for k in offsets:
        t = wrap(me + k, groups)
        anc_copy(t, me).wait_send()
        part_copy(t, me).wait_send()
        tail_copy(t, me).wait_send()
        pick_copy(t, me).wait_send()
    for q in range(half):
        who = 2 * q + inner
        mass_copy(me, who, side_ss).wait_send()

        @pl.when((q <= place) & (place < half - 1))
        def _():
            mass_copy(me, who, up_ss).wait_send()

        @pl.when((q >= place) & (place > 0))
        def _():
            mass_copy(me, who, down_ss).wait_send()


def body(groups, hids, particles, noise, ancestors, accepted, data, targets):
    _, rows_all, width = particles.shape
    depth = rows_all - 2
    rows = depth // groups
    data_rows = data.shape[0]
    padded = -(-data_rows // 128) * 128
    anc = jnp.broadcast_to(ancestors[:, None], (1, 128))
    tail = jnp.concatenate(
        [particles[0, depth:], noise[0, depth:], jnp.zeros((12, width), jnp.bfloat16)], axis=0)
    tgt = jnp.pad(targets, (0, padded - data_rows))[None]
    bf, f32 = jnp.bfloat16, jnp.float32
    vm = pl.BlockSpec(memory_space=pltpu.VMEM)
    anywhere = pl.BlockSpec(memory_space=pl.ANY)
    dma = pltpu.SemaphoreType.DMA
    main, last, fit = pl.pallas_call(
        functools.partial(kernel, groups, hids),
        out_shape=(
            jax.ShapeDtypeStruct((depth, width), bf),
            jax.ShapeDtypeStruct((16, width), bf),
            jax.ShapeDtypeStruct((1, 128), f32),
        ),
        in_specs=[vm, pl.BlockSpec(memory_space=pltpu.SMEM), vm, anywhere, anywhere, vm, vm],
        out_specs=(anywhere, vm, vm),
        scratch_shapes=[
            pltpu.VMEM((groups, 1, 128), jnp.int32),
            pltpu.SMEM((groups, 1, 128), jnp.int32),
            pltpu.VMEM((groups, 16, width), bf),
            pltpu.VMEM((groups, rows, width), bf),
            pltpu.VMEM((groups, rows, width), bf),
            pltpu.VMEM((depth, width), bf),
            pltpu.VMEM((depth, width), bf),
            pltpu.VMEM((depth, width), bf),
            pltpu.VMEM((depth, width), f32),
            pltpu.VMEM((depth, width), f32),
            pltpu.VMEM((depth, width), bf),
            pltpu.VMEM((data_rows, width), f32),
            pltpu.VMEM((data_rows, TILE), f32),
            pltpu.VMEM((16, width), f32),
            pltpu.VMEM((16, width), f32),
            pltpu.VMEM((16, width), f32),
            pltpu.VMEM((16, width), f32),
            pltpu.VMEM((16, width), f32),
            pltpu.VMEM((3, 8, padded), f32),
            pltpu.VMEM((3, hids, 8, padded), f32),
        ] + [dma((groups,))] * 8 + [dma((groups,))] * 4 + [dma((3, hids))] * 2 + [dma((4,))],
        compiler_params=pltpu.CompilerParams(
            collective_id=0, has_side_effects=True, vmem_limit_bytes=56 * 1024 * 1024),
        cost_estimate=pl.CostEstimate(
            flops=10 * data_rows * depth * width, bytes_accessed=8 * depth * width,
            transcendentals=3 * data_rows * width),
    )(anc, accepted, tail, particles, noise, data, tgt)
    moved = jnp.concatenate([main, last[:2]], axis=0)[None]
    return moved, fit[0, :1]


def solution(mesh):
    groups, hids = mesh.shape["dom"], mesh.shape["hid"]
    return jax.shard_map(
        functools.partial(body, groups, hids),
        mesh=mesh,
        in_specs=(P("dom", None, "hid"), P("dom", None, "hid"), P("dom"), P("dom"), P(), P()),
        out_specs=(P("dom", None, "hid"), P("dom")),
        check_vma=False,
    )
```

```python
import functools

import jax
import jax.numpy as jnp
from jax import lax
from jax.experimental import pallas as pl
from jax.experimental.pallas import tpu as pltpu
from jax.sharding import PartitionSpec as P

TEMPER_LEVEL = 0.125
NOISE_INV_VARIANCE = 4.0
STEP_SIZE = 0.4
MESH = pl.DeviceIdType.MESH
TILE = 256
CHUNK = 16
CHUNKS = 2


def kernel(
    groups, hids, chunks,
    anc_ref, acc_ref, part_ref, noise_ref, data_ref, tgt_ref,
    main_out, fit_out,
    anc_all, anc_s, tails, recv, picked, theta0, mass, part_v, noise_v, data_t, mom, pos, moved, hid, resid,
    tgt, tpos, tpos0, tmom, tinv, part_buf, part_all,
    anc_ss, anc_rs, tail_ss, tail_rs, p_ss, p_rs, q_ss, q_rs,
    up_ss, down_ss, side_ss, mass_rs, h_ss, h_rs, loc,
):
    me = lax.axis_index("dom")
    my_hid = lax.axis_index("hid")
    depth, width = theta0.shape
    rows = depth // groups
    piece = rows // chunks
    data_rows = data_ref.shape[0]
    padded = part_buf.shape[-1]
    in_scale = depth ** (-0.5)
    out_scale = (width * hids) ** (-0.5)
    half = groups // 2
    offsets = []
    for s in range(groups - 1):
        offsets.append(half + (s + 1) // 2 * (1 if s % 2 else -1))

    def wrap(i, n):
        return lax.rem(i, n)

    def block(i, ch):
        return pl.ds(pl.multiple_of(i * rows + ch * piece, piece), piece)

    part_load = pltpu.make_async_copy(part_ref.at[0], part_v, loc.at[1])
    part_load.start()
    noise_copy = pltpu.make_async_copy(noise_ref.at[0], noise_v, loc.at[0])
    noise_copy.start()
    anc_all[me] = jnp.full((1, 128), anc_ref[0], jnp.int32)

    barrier = pltpu.get_barrier_semaphore()
    for k in range(1, groups):
        pl.semaphore_signal(barrier, inc=1, device_id=(wrap(me + k, groups), my_hid), device_id_type=MESH)
    for k in range(1, hids):
        pl.semaphore_signal(barrier, inc=1, device_id=(me, wrap(my_hid + k, hids)), device_id_type=MESH)
    pl.semaphore_wait(barrier, groups - 1 + hids - 1)

    def anc_copy(t, slot):
        return pltpu.make_async_remote_copy(
            anc_all.at[slot], anc_all.at[slot], anc_ss.at[t], anc_rs.at[slot],
            device_id=(t, my_hid), device_id_type=MESH)

    def tail_copy(t, slot):
        return pltpu.make_async_remote_copy(
            tails.at[slot], tails.at[slot], tail_ss.at[t], tail_rs.at[slot],
            device_id=(t, my_hid), device_id_type=MESH)

    def local_rows(ch):
        return pl.ds(ch * piece, piece)

    def part_copy(t, slot, ch):
        return pltpu.make_async_remote_copy(
            part_ref.at[0, block(t, ch)], recv[ch].at[slot], p_ss.at[ch, t], p_rs.at[ch, slot],
            device_id=(t, my_hid), device_id_type=MESH)

    def pick_copy(t, slot, ch):
        return pltpu.make_async_remote_copy(
            picked.at[t, local_rows(ch)], theta0.at[block(slot, ch)], q_ss.at[ch, t], q_rs.at[ch, slot],
            device_id=(t, my_hid), device_id_type=MESH)

    for k in offsets:
        anc_copy(wrap(me + k, groups), me).start()
    for ch in range(chunks):
        for k in offsets:
            part_copy(wrap(me + k, groups), me, ch).start()

    data_t[...] = jnp.transpose(data_ref[...].astype(jnp.float32)).astype(jnp.bfloat16)
    tgt[...] = jnp.zeros_like(tgt)
    tgt[:, 0:data_rows] = tgt_ref[...]
    part_load.wait()
    tails[me] = jnp.zeros((16, width), jnp.bfloat16)
    tails[me, 0:2] = part_v[depth:depth + 2]
    for k in offsets:
        tail_copy(wrap(me + k, groups), me).start()
    for ch in range(chunks):
        recv[ch][me] = part_v[block(me, ch)]
    noise_copy.wait()

    for k in offsets:
        s = wrap(me + groups - k, groups)
        anc_copy(s, s).wait_recv()
    scalars = pltpu.make_async_copy(anc_all, anc_s, loc.at[2])
    scalars.start()
    scalars.wait()

    shrink = groups / (groups + 5.0)
    floor_term = 0.001 * 5.0 / (groups + 5.0)

    def finish(total, square):
        mean = total / groups
        return (shrink * (square / groups - mean * mean) + floor_term).astype(jnp.bfloat16)

    for k in offsets:
        s = wrap(me + groups - k, groups)
        tail_copy(s, s).wait_recv()

    def add_tail(i, carry):
        total, square = carry
        wide = tails[anc_s[i, 0, 0]].astype(jnp.float32)
        return total + wide, square + wide * wide

    zero = jnp.zeros((16, width), jnp.float32)
    tinv[...] = finish(*lax.fori_loop(0, groups, add_tail, (zero, zero))).astype(jnp.float32)
    tpos0[...] = tails[anc_s[me, 0, 0]].astype(jnp.float32)
    tpos[...] = tpos0[...]
    tmom[0:2] = noise_v[depth:depth + 2].astype(jnp.float32) * lax.rsqrt(tinv[0:2])

    place, inner = me // 2, lax.rem(me, 2)

    def mass_copy(t, who, ch, sem):
        return pltpu.make_async_remote_copy(
            mass.at[block(who, ch)], mass.at[block(who, ch)], sem.at[ch, who], mass_rs.at[ch, who],
            device_id=(t, my_hid), device_id_type=MESH)

    def spread(who, ch, up, down):
        if up:
            @pl.when(place < half - 1)
            def _():
                mass_copy(me + 2, who, ch, up_ss).start()
        if down:
            @pl.when(place > 0)
            def _():
                mass_copy(me - 2, who, ch, down_ss).start()
        mass_copy(me + 1 - 2 * inner, who, ch, side_ss).start()

    def select(ch):
        for k in offsets:
            s = wrap(me + groups - k, groups)
            part_copy(s, s, ch).wait_recv()

        @pl.loop(0, piece // CHUNK)
        def _(r):
            here = pl.ds(pl.multiple_of(ch * piece + r * CHUNK, CHUNK), CHUNK)

            def add(i, carry):
                total, square = carry
                got = recv[ch][anc_s[i, 0, 0], pl.ds(pl.multiple_of(r * CHUNK, CHUNK), CHUNK)]
                picked[i, here] = got
                wide = got.astype(jnp.float32)
                return total + wide, square + wide * wide

            zero = jnp.zeros((CHUNK, width), jnp.float32)
            carry = (zero, zero)
            if groups <= 8:
                for i in range(groups):
                    carry = add(i, carry)
            else:
                carry = lax.fori_loop(0, groups, add, carry)
            there = pl.ds(pl.multiple_of(me * rows + ch * piece + r * CHUNK, CHUNK), CHUNK)
            mass[there] = finish(*carry)
            theta0[there] = picked[me, here]

        spread(me, ch, True, True)
        for k in offsets:
            pick_copy(wrap(me + k, groups), me, ch).start()

    def forward_mass(s, ch):
        @pl.when(place >= s)
        def _():
            mass_copy(me, me - 2 * s, ch, up_ss).wait_recv()
            spread(me - 2 * s, ch, True, False)

        @pl.when(place + s < half)
        def _():
            mass_copy(me, me + 2 * s, ch, up_ss).wait_recv()
            spread(me + 2 * s, ch, False, True)

    for stage in range(chunks + half - 1):
        if stage < chunks:
            select(stage)
        for s in range(1, half):
            if 0 <= stage - s < chunks:
                forward_mass(s, stage - s)

    for ch in range(chunks):
        for k in offsets:
            s = wrap(me + groups - k, groups)
            pick_copy(s, s, ch).wait_recv()

    def forward(weights, cols, keep_hidden):
        pre = jnp.dot(data_ref[...], weights, preferred_element_type=jnp.float32)
        h = jnp.tanh(pre * in_scale + tpos[0:1, cols])
        if keep_hidden:
            hid[:, cols] = h
        weighted = h * tpos[1:2, cols]
        total = weighted[:, 0:128]
        for c in range(128, TILE, 128):
            total = total + weighted[:, c:c + 128]
        return total

    def tile(c):
        return pl.ds(pl.multiple_of(c * TILE, TILE), TILE)

    none = jnp.zeros((data_rows, 128), jnp.float32)
    tiles = width // TILE

    def outputs(stage, total):
        total = jnp.concatenate([total, jnp.zeros((padded - data_rows, 128), jnp.float32)], axis=0)
        flat = jnp.sum(jnp.transpose(total), axis=0, keepdims=True) * out_scale
        part_buf[stage] = jnp.broadcast_to(flat, (8, padded))

        def copy(t, slot):
            return pltpu.make_async_remote_copy(
                part_buf.at[stage], part_all.at[stage, slot], h_ss.at[stage, t], h_rs.at[stage, slot],
                device_id=(me, t), device_id_type=MESH)

        for k in range(1, hids):
            copy(wrap(my_hid + k, hids), my_hid).start()
        part_all[stage, my_hid] = part_buf[stage]
        for k in range(1, hids):
            s = wrap(my_hid + k, hids)
            copy(s, s).wait_recv()
        for k in range(1, hids):
            copy(wrap(my_hid + k, hids), my_hid).wait_send()
        result = part_all[stage, 0]
        for j in range(1, hids):
            result = result + part_all[stage, j]
        return result[0:1]

    def set_resid(result):
        r = TEMPER_LEVEL * NOISE_INV_VARIANCE * (result - tgt[...])
        column = jnp.transpose(jnp.broadcast_to(r, (128, padded)))[0:data_rows]
        for c in range(0, TILE, 128):
            resid[:, c:c + 128] = column

    keep = acc_ref[0] == 1

    def backward(cols, step):
        h = hid[:, cols]
        b, v = tpos[0:1, cols], tpos[1:2, cols]
        res = resid[...]
        grad_v = jnp.sum(res * h, axis=0, keepdims=True) * out_scale + v
        back = res * (v * out_scale) * (1.0 - h * h)
        grad_b = jnp.sum(back, axis=0, keepdims=True) + b
        grad = jnp.dot(data_t[...], back.astype(jnp.bfloat16), preferred_element_type=jnp.float32) * in_scale
        tm = tmom[0:2, cols] - step * jnp.concatenate([grad_b, grad_v], axis=0)
        tmom[0:2, cols] = tm
        tpos[0:2, cols] = tpos[0:2, cols] + STEP_SIZE * tinv[0:2, cols] * tm
        return grad

    start = lax.fori_loop(
        0, tiles, lambda c, total: total + forward(theta0[:, tile(c)], tile(c), True), none)
    outputs0 = outputs(0, start)
    set_resid(outputs0)

    @pl.loop(0, tiles)
    def _(c):
        cols = tile(c)
        mom[:, cols] = backward(cols, 0.5 * STEP_SIZE) + theta0[:, cols].astype(jnp.float32)

    for ch in range(chunks):
        for q in range(half):
            mass_copy(me, 2 * q + 1 - inner, ch, side_ss).wait_recv()

    def first_move(c, total):
        cols = tile(c)
        inv = mass[:, cols].astype(jnp.float32)
        m = noise_v[0:depth, cols].astype(jnp.float32) * lax.rsqrt(inv) - 0.5 * STEP_SIZE * mom[:, cols]
        w = theta0[:, cols].astype(jnp.float32) + STEP_SIZE * inv * m
        mom[:, cols] = m
        pos[:, cols] = w
        return total + forward(w.astype(jnp.bfloat16), cols, True)

    def last_move(c, total):
        cols = tile(c)
        w = pos[:, cols]
        m = mom[:, cols] - STEP_SIZE * (backward(cols, STEP_SIZE) + w)
        w = w + STEP_SIZE * mass[:, cols].astype(jnp.float32) * m
        moved[0:depth, cols] = jnp.where(keep, w, theta0[:, cols].astype(jnp.float32)).astype(jnp.bfloat16)
        return total + forward(w.astype(jnp.bfloat16), cols, False)

    set_resid(outputs(1, lax.fori_loop(0, tiles, first_move, none)))
    last = lax.fori_loop(0, tiles, last_move, none)
    moved[depth:depth + 2] = jnp.where(keep, tpos[0:2], tpos0[0:2]).astype(jnp.bfloat16)
    result_copy = pltpu.make_async_copy(moved, main_out.at[0], loc.at[3])
    result_copy.start()
    outputs2 = outputs(2, last)
    miss = tgt[...] - jnp.where(keep, outputs2, outputs0)
    fit_out[...] = jnp.broadcast_to(jnp.sum(miss * miss, axis=1, keepdims=True) / data_rows, fit_out.shape)

    result_copy.wait()
    for k in offsets:
        t = wrap(me + k, groups)
        anc_copy(t, me).wait_send()
        tail_copy(t, me).wait_send()
    for ch in range(chunks):
        for k in offsets:
            t = wrap(me + k, groups)
            part_copy(t, me, ch).wait_send()
            pick_copy(t, me, ch).wait_send()
        for q in range(half):
            who = 2 * q + inner
            mass_copy(me, who, ch, side_ss).wait_send()

            @pl.when((q <= place) & (place < half - 1))
            def _():
                mass_copy(me, who, ch, up_ss).wait_send()

            @pl.when((q >= place) & (place > 0))
            def _():
                mass_copy(me, who, ch, down_ss).wait_send()


def body(groups, hids, particles, noise, ancestors, accepted, data, targets):
    _, rows_all, width = particles.shape
    depth = rows_all - 2
    rows = depth // groups
    chunks = min(CHUNKS, rows // CHUNK)
    data_rows = data.shape[0]
    padded = -(-data_rows // 128) * 128
    bf, f32 = jnp.bfloat16, jnp.float32
    vm = pl.BlockSpec(memory_space=pltpu.VMEM)
    sm = pl.BlockSpec(memory_space=pltpu.SMEM)
    anywhere = pl.BlockSpec(memory_space=pl.ANY)
    dma = pltpu.SemaphoreType.DMA
    moved, fit = pl.pallas_call(
        functools.partial(kernel, groups, hids, chunks),
        out_shape=(
            jax.ShapeDtypeStruct((1, rows_all, width), bf),
            jax.ShapeDtypeStruct((1, 128), f32),
        ),
        in_specs=[sm, sm, anywhere, anywhere, vm, vm],
        out_specs=(anywhere, vm),
        scratch_shapes=[
            pltpu.VMEM((groups, 1, 128), jnp.int32),
            pltpu.SMEM((groups, 1, 128), jnp.int32),
            pltpu.VMEM((groups, 16, width), bf),
            [pltpu.VMEM((groups, rows // chunks, width), bf)] * chunks,
            pltpu.VMEM((groups, rows, width), bf),
            pltpu.VMEM((depth, width), bf),
            pltpu.VMEM((depth, width), bf),
            pltpu.VMEM((rows_all, width), bf),
            pltpu.VMEM((rows_all, width), bf),
            pltpu.VMEM((depth, data_rows), bf),
            pltpu.VMEM((depth, width), f32),
            pltpu.VMEM((depth, width), f32),
            pltpu.VMEM((rows_all, width), bf),
            pltpu.VMEM((data_rows, width), f32),
            pltpu.VMEM((data_rows, TILE), f32),
            pltpu.VMEM((1, padded), f32),
            pltpu.VMEM((16, width), f32),
            pltpu.VMEM((16, width), f32),
            pltpu.VMEM((16, width), f32),
            pltpu.VMEM((16, width), f32),
            pltpu.VMEM((3, 8, padded), f32),
            pltpu.VMEM((3, hids, 8, padded), f32),
        ] + [dma((groups,))] * 4 + [dma((chunks, groups))] * 8 + [dma((3, hids))] * 2 + [dma((4,))],
        compiler_params=pltpu.CompilerParams(
            collective_id=0, has_side_effects=True, vmem_limit_bytes=56 * 1024 * 1024),
        cost_estimate=pl.CostEstimate(
            flops=10 * data_rows * depth * width, bytes_accessed=8 * depth * width,
            transcendentals=3 * data_rows * width),
    )(ancestors, accepted, particles, noise, data, targets[None])
    return moved, fit[0, :1]


def solution(mesh):
    groups, hids = mesh.shape["dom"], mesh.shape["hid"]
    return jax.shard_map(
        functools.partial(body, groups, hids),
        mesh=mesh,
        in_specs=(P("dom", None, "hid"), P("dom", None, "hid"), P("dom"), P("dom"), P(), P()),
        out_specs=(P("dom", None, "hid"), P("dom")),
        check_vma=False,
    )
```

```python
import functools

import jax
import jax.numpy as jnp
from jax import lax
from jax.experimental import pallas as pl
from jax.experimental.pallas import tpu as pltpu
from jax.sharding import PartitionSpec as P

TEMPER_LEVEL = 0.125
NOISE_INV_VARIANCE = 4.0
STEP_SIZE = 0.4
MESH = pl.DeviceIdType.MESH
TILE = 256
CHUNK = 16
CHUNKS = 2


def kernel(
    groups, hids, chunks,
    anc_ref, acc_ref, part_ref, noise_ref, data_ref, tgt_ref,
    main_out, fit_out,
    anc_all, anc_s, tails, recv, picked, theta0, mass, part_v, noise_v, data_t, mom, pos, moved, hid, resid,
    tgt, tpos, tpos0, tmom, tinv, part_buf, part_all,
    anc_ss, anc_rs, tail_ss, tail_rs, p_ss, p_rs, q_ss, q_rs,
    up_ss, down_ss, side_ss, mass_rs, h_ss, h_rs, loc,
):
    me = lax.axis_index("dom")
    my_hid = lax.axis_index("hid")
    depth, width = theta0.shape
    rows = depth // groups
    piece = rows // chunks
    data_rows = data_ref.shape[0]
    padded = part_buf.shape[-1]
    in_scale = depth ** (-0.5)
    out_scale = (width * hids) ** (-0.5)
    half = groups // 2
    offsets = []
    for s in range(groups - 1):
        offsets.append(half + (s + 1) // 2 * (1 if s % 2 else -1))

    def wrap(i, n):
        return lax.rem(i, n)

    def block(i, ch):
        return pl.ds(pl.multiple_of(i * rows + ch * piece, piece), piece)

    part_load = pltpu.make_async_copy(part_ref.at[0], part_v, loc.at[1])
    part_load.start()
    noise_copy = pltpu.make_async_copy(noise_ref.at[0], noise_v, loc.at[0])
    noise_copy.start()
    anc_all[me] = jnp.full((1, 128), anc_ref[0], jnp.int32)

    barrier = pltpu.get_barrier_semaphore()
    for k in range(1, groups):
        pl.semaphore_signal(barrier, inc=1, device_id=(wrap(me + k, groups), my_hid), device_id_type=MESH)
    for k in range(1, hids):
        pl.semaphore_signal(barrier, inc=1, device_id=(me, wrap(my_hid + k, hids)), device_id_type=MESH)
    pl.semaphore_wait(barrier, groups - 1 + hids - 1)

    def anc_copy(t, slot):
        return pltpu.make_async_remote_copy(
            anc_all.at[slot], anc_all.at[slot], anc_ss.at[t], anc_rs.at[slot],
            device_id=(t, my_hid), device_id_type=MESH)

    def tail_copy(t, slot):
        return pltpu.make_async_remote_copy(
            tails.at[slot], tails.at[slot], tail_ss.at[t], tail_rs.at[slot],
            device_id=(t, my_hid), device_id_type=MESH)

    def local_rows(ch):
        return pl.ds(ch * piece, piece)

    def part_copy(t, slot, ch):
        return pltpu.make_async_remote_copy(
            part_ref.at[0, block(t, ch)], recv[ch].at[slot], p_ss.at[ch, t], p_rs.at[ch, slot],
            device_id=(t, my_hid), device_id_type=MESH)

    def pick_copy(t, slot, ch):
        return pltpu.make_async_remote_copy(
            picked.at[t, local_rows(ch)], theta0.at[block(slot, ch)], q_ss.at[ch, t], q_rs.at[ch, slot],
            device_id=(t, my_hid), device_id_type=MESH)

    for k in offsets:
        anc_copy(wrap(me + k, groups), me).start()
    for ch in range(chunks):
        for k in offsets:
            part_copy(wrap(me + k, groups), me, ch).start()

    data_t[...] = jnp.transpose(data_ref[...].astype(jnp.float32)).astype(jnp.bfloat16)
    tgt[...] = jnp.zeros_like(tgt)
    tgt[:, 0:data_rows] = tgt_ref[...]
    part_load.wait()
    tails[me] = jnp.zeros((16, width), jnp.bfloat16)
    tails[me, 0:2] = part_v[depth:depth + 2]
    for k in offsets:
        tail_copy(wrap(me + k, groups), me).start()
    for ch in range(chunks):
        recv[ch][me] = part_v[block(me, ch)]
    noise_copy.wait()

    for k in offsets:
        s = wrap(me + groups - k, groups)
        anc_copy(s, s).wait_recv()
    scalars = pltpu.make_async_copy(anc_all, anc_s, loc.at[2])
    scalars.start()
    scalars.wait()

    shrink = groups / (groups + 5.0)
    floor_term = 0.001 * 5.0 / (groups + 5.0)

    def finish(total, square):
        mean = total / groups
        return (shrink * (square / groups - mean * mean) + floor_term).astype(jnp.bfloat16)

    for k in offsets:
        s = wrap(me + groups - k, groups)
        tail_copy(s, s).wait_recv()

    def add_tail(i, carry):
        total, square = carry
        wide = tails[anc_s[i, 0, 0]].astype(jnp.float32)
        return total + wide, square + wide * wide

    zero = jnp.zeros((16, width), jnp.float32)
    tinv[...] = finish(*lax.fori_loop(0, groups, add_tail, (zero, zero))).astype(jnp.float32)
    tpos0[...] = tails[anc_s[me, 0, 0]].astype(jnp.float32)
    tpos[...] = tpos0[...]
    tmom[0:2] = noise_v[depth:depth + 2].astype(jnp.float32) * lax.rsqrt(tinv[0:2])

    place, inner = me // 2, lax.rem(me, 2)

    def mass_copy(t, who, ch, sem):
        return pltpu.make_async_remote_copy(
            mass.at[block(who, ch)], mass.at[block(who, ch)], sem.at[ch, who], mass_rs.at[ch, who],
            device_id=(t, my_hid), device_id_type=MESH)

    def spread(who, ch, up, down):
        if up:
            @pl.when(place < half - 1)
            def _():
                mass_copy(me + 2, who, ch, up_ss).start()
        if down:
            @pl.when(place > 0)
            def _():
                mass_copy(me - 2, who, ch, down_ss).start()
        mass_copy(me + 1 - 2 * inner, who, ch, side_ss).start()

    def select(ch):
        for k in offsets:
            s = wrap(me + groups - k, groups)
            part_copy(s, s, ch).wait_recv()

        @pl.loop(0, piece // CHUNK)
        def _(r):
            here = pl.ds(pl.multiple_of(ch * piece + r * CHUNK, CHUNK), CHUNK)

            def add(i, carry):
                total, square = carry
                got = recv[ch][anc_s[i, 0, 0], pl.ds(pl.multiple_of(r * CHUNK, CHUNK), CHUNK)]
                picked[i, here] = got
                wide = got.astype(jnp.float32)
                return total + wide, square + wide * wide

            zero = jnp.zeros((CHUNK, width), jnp.float32)
            carry = (zero, zero)
            if groups <= 8:
                for i in range(groups):
                    carry = add(i, carry)
            else:
                carry = lax.fori_loop(0, groups, add, carry)
            there = pl.ds(pl.multiple_of(me * rows + ch * piece + r * CHUNK, CHUNK), CHUNK)
            mass[there] = finish(*carry)
            theta0[there] = picked[me, here]

        spread(me, ch, True, True)

    def forward_mass(s, ch):
        @pl.when(place >= s)
        def _():
            mass_copy(me, me - 2 * s, ch, up_ss).wait_recv()
            spread(me - 2 * s, ch, True, False)

        @pl.when(place + s < half)
        def _():
            mass_copy(me, me + 2 * s, ch, up_ss).wait_recv()
            spread(me + 2 * s, ch, False, True)

    stages = chunks + half - 1
    pending = []
    quota = -(-chunks * (groups - 1) // stages)
    for stage in range(stages):
        if stage < chunks:
            select(stage)
            pending += [(k, stage) for k in offsets]
        for k, ch in pending[:quota]:
            pick_copy(wrap(me + k, groups), me, ch).start()
        pending = pending[quota:]
        for s in range(1, half):
            if 0 <= stage - s < chunks:
                forward_mass(s, stage - s)

    for ch in range(chunks):
        for k in offsets:
            s = wrap(me + groups - k, groups)
            pick_copy(s, s, ch).wait_recv()

    def forward(weights, cols, keep_hidden):
        pre = jnp.dot(data_ref[...], weights, preferred_element_type=jnp.float32)
        h = jnp.tanh(pre * in_scale + tpos[0:1, cols])
        if keep_hidden:
            hid[:, cols] = h
        weighted = h * tpos[1:2, cols]
        total = weighted[:, 0:128]
        for c in range(128, TILE, 128):
            total = total + weighted[:, c:c + 128]
        return total

    def tile(c):
        return pl.ds(pl.multiple_of(c * TILE, TILE), TILE)

    none = jnp.zeros((data_rows, 128), jnp.float32)
    tiles = width // TILE

    def outputs(stage, total):
        total = jnp.concatenate([total, jnp.zeros((padded - data_rows, 128), jnp.float32)], axis=0)
        flat = jnp.sum(jnp.transpose(total), axis=0, keepdims=True) * out_scale
        part_buf[stage] = jnp.broadcast_to(flat, (8, padded))

        def copy(t, slot):
            return pltpu.make_async_remote_copy(
                part_buf.at[stage], part_all.at[stage, slot], h_ss.at[stage, t], h_rs.at[stage, slot],
                device_id=(me, t), device_id_type=MESH)

        for k in range(1, hids):
            copy(wrap(my_hid + k, hids), my_hid).start()
        part_all[stage, my_hid] = part_buf[stage]
        for k in range(1, hids):
            s = wrap(my_hid + k, hids)
            copy(s, s).wait_recv()
        for k in range(1, hids):
            copy(wrap(my_hid + k, hids), my_hid).wait_send()
        result = part_all[stage, 0]
        for j in range(1, hids):
            result = result + part_all[stage, j]
        return result[0:1]

    def set_resid(result):
        r = TEMPER_LEVEL * NOISE_INV_VARIANCE * (result - tgt[...])
        column = jnp.transpose(jnp.broadcast_to(r, (128, padded)))[0:data_rows]
        for c in range(0, TILE, 128):
            resid[:, c:c + 128] = column

    keep = acc_ref[0] == 1

    def backward(cols, step):
        h = hid[:, cols]
        b, v = tpos[0:1, cols], tpos[1:2, cols]
        res = resid[...]
        grad_v = jnp.sum(res * h, axis=0, keepdims=True) * out_scale + v
        back = res * (v * out_scale) * (1.0 - h * h)
        grad_b = jnp.sum(back, axis=0, keepdims=True) + b
        grad = jnp.dot(data_t[...], back.astype(jnp.bfloat16), preferred_element_type=jnp.float32) * in_scale
        tm = tmom[0:2, cols] - step * jnp.concatenate([grad_b, grad_v], axis=0)
        tmom[0:2, cols] = tm
        tpos[0:2, cols] = tpos[0:2, cols] + STEP_SIZE * tinv[0:2, cols] * tm
        return grad

    start = lax.fori_loop(
        0, tiles, lambda c, total: total + forward(theta0[:, tile(c)], tile(c), True), none)
    outputs0 = outputs(0, start)
    set_resid(outputs0)

    @pl.loop(0, tiles)
    def _(c):
        cols = tile(c)
        mom[:, cols] = backward(cols, 0.5 * STEP_SIZE) + theta0[:, cols].astype(jnp.float32)

    for ch in range(chunks):
        for q in range(half):
            mass_copy(me, 2 * q + 1 - inner, ch, side_ss).wait_recv()

    def first_move(c, total):
        cols = tile(c)
        inv = mass[:, cols].astype(jnp.float32)
        m = noise_v[0:depth, cols].astype(jnp.float32) * lax.rsqrt(inv) - 0.5 * STEP_SIZE * mom[:, cols]
        w = theta0[:, cols].astype(jnp.float32) + STEP_SIZE * inv * m
        mom[:, cols] = m
        pos[:, cols] = w
        return total + forward(w.astype(jnp.bfloat16), cols, True)

    def last_move(c, total):
        cols = tile(c)
        w = pos[:, cols]
        m = mom[:, cols] - STEP_SIZE * (backward(cols, STEP_SIZE) + w)
        w = w + STEP_SIZE * mass[:, cols].astype(jnp.float32) * m
        moved[0:depth, cols] = jnp.where(keep, w, theta0[:, cols].astype(jnp.float32)).astype(jnp.bfloat16)
        return total + forward(w.astype(jnp.bfloat16), cols, False)

    set_resid(outputs(1, lax.fori_loop(0, tiles, first_move, none)))
    last = lax.fori_loop(0, tiles, last_move, none)
    moved[depth:depth + 2] = jnp.where(keep, tpos[0:2], tpos0[0:2]).astype(jnp.bfloat16)
    result_copy = pltpu.make_async_copy(moved, main_out.at[0], loc.at[3])
    result_copy.start()
    outputs2 = outputs(2, last)
    miss = tgt[...] - jnp.where(keep, outputs2, outputs0)
    fit_out[...] = jnp.broadcast_to(jnp.sum(miss * miss, axis=1, keepdims=True) / data_rows, fit_out.shape)

    result_copy.wait()
    for k in offsets:
        t = wrap(me + k, groups)
        anc_copy(t, me).wait_send()
        tail_copy(t, me).wait_send()
    for ch in range(chunks):
        for k in offsets:
            t = wrap(me + k, groups)
            part_copy(t, me, ch).wait_send()
            pick_copy(t, me, ch).wait_send()
        for q in range(half):
            who = 2 * q + inner
            mass_copy(me, who, ch, side_ss).wait_send()

            @pl.when((q <= place) & (place < half - 1))
            def _():
                mass_copy(me, who, ch, up_ss).wait_send()

            @pl.when((q >= place) & (place > 0))
            def _():
                mass_copy(me, who, ch, down_ss).wait_send()


def body(groups, hids, particles, noise, ancestors, accepted, data, targets):
    _, rows_all, width = particles.shape
    depth = rows_all - 2
    rows = depth // groups
    chunks = min(CHUNKS, rows // CHUNK)
    data_rows = data.shape[0]
    padded = -(-data_rows // 128) * 128
    bf, f32 = jnp.bfloat16, jnp.float32
    vm = pl.BlockSpec(memory_space=pltpu.VMEM)
    sm = pl.BlockSpec(memory_space=pltpu.SMEM)
    anywhere = pl.BlockSpec(memory_space=pl.ANY)
    dma = pltpu.SemaphoreType.DMA
    moved, fit = pl.pallas_call(
        functools.partial(kernel, groups, hids, chunks),
        out_shape=(
            jax.ShapeDtypeStruct((1, rows_all, width), bf),
            jax.ShapeDtypeStruct((1, 128), f32),
        ),
        in_specs=[sm, sm, anywhere, anywhere, vm, vm],
        out_specs=(anywhere, vm),
        scratch_shapes=[
            pltpu.VMEM((groups, 1, 128), jnp.int32),
            pltpu.SMEM((groups, 1, 128), jnp.int32),
            pltpu.VMEM((groups, 16, width), bf),
            [pltpu.VMEM((groups, rows // chunks, width), bf)] * chunks,
            pltpu.VMEM((groups, rows, width), bf),
            pltpu.VMEM((depth, width), bf),
            pltpu.VMEM((depth, width), bf),
            pltpu.VMEM((rows_all, width), bf),
            pltpu.VMEM((rows_all, width), bf),
            pltpu.VMEM((depth, data_rows), bf),
            pltpu.VMEM((depth, width), f32),
            pltpu.VMEM((depth, width), f32),
            pltpu.VMEM((rows_all, width), bf),
            pltpu.VMEM((data_rows, width), f32),
            pltpu.VMEM((data_rows, TILE), f32),
            pltpu.VMEM((1, padded), f32),
            pltpu.VMEM((16, width), f32),
            pltpu.VMEM((16, width), f32),
            pltpu.VMEM((16, width), f32),
            pltpu.VMEM((16, width), f32),
            pltpu.VMEM((3, 8, padded), f32),
            pltpu.VMEM((3, hids, 8, padded), f32),
        ] + [dma((groups,))] * 4 + [dma((chunks, groups))] * 8 + [dma((3, hids))] * 2 + [dma((4,))],
        compiler_params=pltpu.CompilerParams(
            collective_id=0, has_side_effects=True, vmem_limit_bytes=56 * 1024 * 1024),
        cost_estimate=pl.CostEstimate(
            flops=10 * data_rows * depth * width, bytes_accessed=8 * depth * width,
            transcendentals=3 * data_rows * width),
    )(ancestors, accepted, particles, noise, data, targets[None])
    return moved, fit[0, :1]


def solution(mesh):
    groups, hids = mesh.shape["dom"], mesh.shape["hid"]
    return jax.shard_map(
        functools.partial(body, groups, hids),
        mesh=mesh,
        in_specs=(P("dom", None, "hid"), P("dom", None, "hid"), P("dom"), P("dom"), P(), P()),
        out_specs=(P("dom", None, "hid"), P("dom")),
        check_vma=False,
    )
```

```python
import functools

import jax
import jax.numpy as jnp
from jax import lax
from jax.experimental import pallas as pl
from jax.experimental.pallas import tpu as pltpu
from jax.sharding import PartitionSpec as P

TEMPER_LEVEL = 0.125
NOISE_INV_VARIANCE = 4.0
STEP_SIZE = 0.4
MESH = pl.DeviceIdType.MESH
TILE = 256
CHUNK = 16
CHUNKS = 2


def kernel(
    groups, hids, chunks,
    anc_ref, acc_ref, part_ref, noise_ref, data_ref, tgt_ref,
    main_out, fit_out,
    anc_all, anc_s, tails, recv, picked, theta0, mass, part_v, noise_v, data_t, mom, pos, moved, hid, resid,
    tgt, tpos, tpos0, tmom, tinv, part_buf, part_all,
    anc_ss, anc_rs, tail_ss, tail_rs, p_ss, p_rs, q_ss, q_rs,
    up_ss, down_ss, side_ss, mass_rs, h_ss, h_rs, loc,
):
    me = lax.axis_index("dom")
    my_hid = lax.axis_index("hid")
    depth, width = theta0.shape
    rows = depth // groups
    piece = rows // chunks
    data_rows = data_ref.shape[0]
    padded = part_buf.shape[-1]
    in_scale = depth ** (-0.5)
    out_scale = (width * hids) ** (-0.5)
    half = groups // 2
    offsets = range(1, groups)
    far, near = list(range(half, groups)), list(range(1, half))
    far_first = [m for pair in zip(far, near) for m in pair] + far[half - 1:]
    near_first = [m for pair in zip(near, far) for m in pair] + far[half - 1:]

    def flip(m):
        t = me
        for bit in range(groups.bit_length() - 1):
            if m >> bit & 1:
                t = t + (1 << bit) - 2 * (1 << bit) * lax.rem(me // (1 << bit), 2)
        return t

    def target(s):
        odd = lax.rem(me // 2, 2)
        first, second = flip(far_first[s]), flip(near_first[s])
        return first + odd * (second - first)

    def wrap(i, n):
        return lax.rem(i, n)

    def block(i, ch):
        return pl.ds(pl.multiple_of(i * rows + ch * piece, piece), piece)

    part_load = pltpu.make_async_copy(part_ref.at[0], part_v, loc.at[1])
    part_load.start()
    noise_copy = pltpu.make_async_copy(noise_ref.at[0], noise_v, loc.at[0])
    noise_copy.start()
    anc_all[me] = jnp.full((1, 128), anc_ref[0], jnp.int32)

    barrier = pltpu.get_barrier_semaphore()
    for k in range(1, groups):
        pl.semaphore_signal(barrier, inc=1, device_id=(wrap(me + k, groups), my_hid), device_id_type=MESH)
    for k in range(1, hids):
        pl.semaphore_signal(barrier, inc=1, device_id=(me, wrap(my_hid + k, hids)), device_id_type=MESH)
    pl.semaphore_wait(barrier, groups - 1 + hids - 1)

    def anc_copy(t, slot):
        return pltpu.make_async_remote_copy(
            anc_all.at[slot], anc_all.at[slot], anc_ss.at[t], anc_rs.at[slot],
            device_id=(t, my_hid), device_id_type=MESH)

    def tail_copy(t, slot):
        return pltpu.make_async_remote_copy(
            tails.at[slot], tails.at[slot], tail_ss.at[t], tail_rs.at[slot],
            device_id=(t, my_hid), device_id_type=MESH)

    def local_rows(ch):
        return pl.ds(ch * piece, piece)

    def part_copy(t, slot, ch):
        return pltpu.make_async_remote_copy(
            part_ref.at[0, block(t, ch)], recv[ch].at[slot], p_ss.at[ch, t], p_rs.at[ch, slot],
            device_id=(t, my_hid), device_id_type=MESH)

    def pick_copy(t, slot, ch):
        return pltpu.make_async_remote_copy(
            picked.at[t, local_rows(ch)], theta0.at[block(slot, ch)], q_ss.at[ch, t], q_rs.at[ch, slot],
            device_id=(t, my_hid), device_id_type=MESH)

    for k in offsets:
        anc_copy(wrap(me + k, groups), me).start()
    for ch in range(chunks):
        for s in range(groups - 1):
            part_copy(target(s), me, ch).start()

    data_t[...] = jnp.transpose(data_ref[...].astype(jnp.float32)).astype(jnp.bfloat16)
    tgt[...] = jnp.zeros_like(tgt)
    tgt[:, 0:data_rows] = tgt_ref[...]
    part_load.wait()
    tails[me] = jnp.zeros((16, width), jnp.bfloat16)
    tails[me, 0:2] = part_v[depth:depth + 2]
    for k in offsets:
        tail_copy(wrap(me + k, groups), me).start()
    for ch in range(chunks):
        recv[ch][me] = part_v[block(me, ch)]
    noise_copy.wait()

    for k in offsets:
        s = wrap(me + groups - k, groups)
        anc_copy(s, s).wait_recv()
    scalars = pltpu.make_async_copy(anc_all, anc_s, loc.at[2])
    scalars.start()
    scalars.wait()

    shrink = groups / (groups + 5.0)
    floor_term = 0.001 * 5.0 / (groups + 5.0)

    def finish(total, square):
        mean = total / groups
        return (shrink * (square / groups - mean * mean) + floor_term).astype(jnp.bfloat16)

    for k in offsets:
        s = wrap(me + groups - k, groups)
        tail_copy(s, s).wait_recv()

    def add_tail(i, carry):
        total, square = carry
        wide = tails[anc_s[i, 0, 0]].astype(jnp.float32)
        return total + wide, square + wide * wide

    zero = jnp.zeros((16, width), jnp.float32)
    tinv[...] = finish(*lax.fori_loop(0, groups, add_tail, (zero, zero))).astype(jnp.float32)
    tpos0[...] = tails[anc_s[me, 0, 0]].astype(jnp.float32)
    tpos[...] = tpos0[...]
    tmom[0:2] = noise_v[depth:depth + 2].astype(jnp.float32) * lax.rsqrt(tinv[0:2])

    place, inner = me // 2, lax.rem(me, 2)

    def mass_copy(t, who, ch, sem):
        return pltpu.make_async_remote_copy(
            mass.at[block(who, ch)], mass.at[block(who, ch)], sem.at[ch, who], mass_rs.at[ch, who],
            device_id=(t, my_hid), device_id_type=MESH)

    def spread(who, ch, up, down):
        if up:
            @pl.when(place < half - 1)
            def _():
                mass_copy(me + 2, who, ch, up_ss).start()
        if down:
            @pl.when(place > 0)
            def _():
                mass_copy(me - 2, who, ch, down_ss).start()
        mass_copy(me + 1 - 2 * inner, who, ch, side_ss).start()

    def select(ch):
        for k in offsets:
            s = wrap(me + groups - k, groups)
            part_copy(s, s, ch).wait_recv()

        @pl.loop(0, piece // CHUNK)
        def _(r):
            here = pl.ds(pl.multiple_of(ch * piece + r * CHUNK, CHUNK), CHUNK)

            def add(i, carry):
                total, square = carry
                got = recv[ch][anc_s[i, 0, 0], pl.ds(pl.multiple_of(r * CHUNK, CHUNK), CHUNK)]
                picked[i, here] = got
                wide = got.astype(jnp.float32)
                return total + wide, square + wide * wide

            zero = jnp.zeros((CHUNK, width), jnp.float32)
            carry = (zero, zero)
            if groups <= 8:
                for i in range(groups):
                    carry = add(i, carry)
            else:
                carry = lax.fori_loop(0, groups, add, carry)
            there = pl.ds(pl.multiple_of(me * rows + ch * piece + r * CHUNK, CHUNK), CHUNK)
            mass[there] = finish(*carry)
            theta0[there] = picked[me, here]

        spread(me, ch, True, True)

    def forward_mass(s, ch):
        @pl.when(place >= s)
        def _():
            mass_copy(me, me - 2 * s, ch, up_ss).wait_recv()
            spread(me - 2 * s, ch, True, False)

        @pl.when(place + s < half)
        def _():
            mass_copy(me, me + 2 * s, ch, up_ss).wait_recv()
            spread(me + 2 * s, ch, False, True)

    stages = chunks + half - 1
    pending = []
    quota = -(-chunks * (groups - 1) // stages)
    for stage in range(stages):
        if stage < chunks:
            select(stage)
            pending += [(s, stage) for s in range(groups - 1)]
        for s, ch in pending[:quota]:
            pick_copy(target(s), me, ch).start()
        pending = pending[quota:]
        for s in range(1, half):
            if 0 <= stage - s < chunks:
                forward_mass(s, stage - s)

    for ch in range(chunks):
        for k in offsets:
            s = wrap(me + groups - k, groups)
            pick_copy(s, s, ch).wait_recv()

    def forward(weights, cols, keep_hidden):
        pre = jnp.dot(data_ref[...], weights, preferred_element_type=jnp.float32)
        h = jnp.tanh(pre * in_scale + tpos[0:1, cols])
        if keep_hidden:
            hid[:, cols] = h
        weighted = h * tpos[1:2, cols]
        total = weighted[:, 0:128]
        for c in range(128, TILE, 128):
            total = total + weighted[:, c:c + 128]
        return total

    def tile(c):
        return pl.ds(pl.multiple_of(c * TILE, TILE), TILE)

    none = jnp.zeros((data_rows, 128), jnp.float32)
    tiles = width // TILE

    def outputs(stage, total):
        total = jnp.concatenate([total, jnp.zeros((padded - data_rows, 128), jnp.float32)], axis=0)
        flat = jnp.sum(jnp.transpose(total), axis=0, keepdims=True) * out_scale
        part_buf[stage] = jnp.broadcast_to(flat, (8, padded))

        def copy(t, slot):
            return pltpu.make_async_remote_copy(
                part_buf.at[stage], part_all.at[stage, slot], h_ss.at[stage, t], h_rs.at[stage, slot],
                device_id=(me, t), device_id_type=MESH)

        for k in range(1, hids):
            copy(wrap(my_hid + k, hids), my_hid).start()
        part_all[stage, my_hid] = part_buf[stage]
        for k in range(1, hids):
            s = wrap(my_hid + k, hids)
            copy(s, s).wait_recv()
        for k in range(1, hids):
            copy(wrap(my_hid + k, hids), my_hid).wait_send()
        result = part_all[stage, 0]
        for j in range(1, hids):
            result = result + part_all[stage, j]
        return result[0:1]

    def set_resid(result):
        r = TEMPER_LEVEL * NOISE_INV_VARIANCE * (result - tgt[...])
        column = jnp.transpose(jnp.broadcast_to(r, (128, padded)))[0:data_rows]
        for c in range(0, TILE, 128):
            resid[:, c:c + 128] = column

    keep = acc_ref[0] == 1

    def backward(cols, step):
        h = hid[:, cols]
        b, v = tpos[0:1, cols], tpos[1:2, cols]
        res = resid[...]
        grad_v = jnp.sum(res * h, axis=0, keepdims=True) * out_scale + v
        back = res * (v * out_scale) * (1.0 - h * h)
        grad_b = jnp.sum(back, axis=0, keepdims=True) + b
        grad = jnp.dot(data_t[...], back.astype(jnp.bfloat16), preferred_element_type=jnp.float32) * in_scale
        tm = tmom[0:2, cols] - step * jnp.concatenate([grad_b, grad_v], axis=0)
        tmom[0:2, cols] = tm
        tpos[0:2, cols] = tpos[0:2, cols] + STEP_SIZE * tinv[0:2, cols] * tm
        return grad

    start = lax.fori_loop(
        0, tiles, lambda c, total: total + forward(theta0[:, tile(c)], tile(c), True), none)
    outputs0 = outputs(0, start)
    set_resid(outputs0)

    @pl.loop(0, tiles)
    def _(c):
        cols = tile(c)
        mom[:, cols] = backward(cols, 0.5 * STEP_SIZE) + theta0[:, cols].astype(jnp.float32)

    for ch in range(chunks):
        for q in range(half):
            mass_copy(me, 2 * q + 1 - inner, ch, side_ss).wait_recv()

    def first_move(c, total):
        cols = tile(c)
        inv = mass[:, cols].astype(jnp.float32)
        m = noise_v[0:depth, cols].astype(jnp.float32) * lax.rsqrt(inv) - 0.5 * STEP_SIZE * mom[:, cols]
        w = theta0[:, cols].astype(jnp.float32) + STEP_SIZE * inv * m
        mom[:, cols] = m
        pos[:, cols] = w
        return total + forward(w.astype(jnp.bfloat16), cols, True)

    def last_move(c, total):
        cols = tile(c)
        w = pos[:, cols]
        m = mom[:, cols] - STEP_SIZE * (backward(cols, STEP_SIZE) + w)
        w = w + STEP_SIZE * mass[:, cols].astype(jnp.float32) * m
        moved[0:depth, cols] = jnp.where(keep, w, theta0[:, cols].astype(jnp.float32)).astype(jnp.bfloat16)
        return total + forward(w.astype(jnp.bfloat16), cols, False)

    set_resid(outputs(1, lax.fori_loop(0, tiles, first_move, none)))
    last = lax.fori_loop(0, tiles, last_move, none)
    moved[depth:depth + 2] = jnp.where(keep, tpos[0:2], tpos0[0:2]).astype(jnp.bfloat16)
    result_copy = pltpu.make_async_copy(moved, main_out.at[0], loc.at[3])
    result_copy.start()
    outputs2 = outputs(2, last)
    miss = tgt[...] - jnp.where(keep, outputs2, outputs0)
    fit_out[...] = jnp.broadcast_to(jnp.sum(miss * miss, axis=1, keepdims=True) / data_rows, fit_out.shape)

    result_copy.wait()
    for k in offsets:
        t = wrap(me + k, groups)
        anc_copy(t, me).wait_send()
        tail_copy(t, me).wait_send()
    for ch in range(chunks):
        for k in offsets:
            t = wrap(me + k, groups)
            part_copy(t, me, ch).wait_send()
            pick_copy(t, me, ch).wait_send()
        for q in range(half):
            who = 2 * q + inner
            mass_copy(me, who, ch, side_ss).wait_send()

            @pl.when((q <= place) & (place < half - 1))
            def _():
                mass_copy(me, who, ch, up_ss).wait_send()

            @pl.when((q >= place) & (place > 0))
            def _():
                mass_copy(me, who, ch, down_ss).wait_send()


def body(groups, hids, particles, noise, ancestors, accepted, data, targets):
    _, rows_all, width = particles.shape
    depth = rows_all - 2
    rows = depth // groups
    chunks = min(CHUNKS, rows // CHUNK)
    data_rows = data.shape[0]
    padded = -(-data_rows // 128) * 128
    bf, f32 = jnp.bfloat16, jnp.float32
    vm = pl.BlockSpec(memory_space=pltpu.VMEM)
    sm = pl.BlockSpec(memory_space=pltpu.SMEM)
    anywhere = pl.BlockSpec(memory_space=pl.ANY)
    dma = pltpu.SemaphoreType.DMA
    moved, fit = pl.pallas_call(
        functools.partial(kernel, groups, hids, chunks),
        out_shape=(
            jax.ShapeDtypeStruct((1, rows_all, width), bf),
            jax.ShapeDtypeStruct((1, 128), f32),
        ),
        in_specs=[sm, sm, anywhere, anywhere, vm, vm],
        out_specs=(anywhere, vm),
        scratch_shapes=[
            pltpu.VMEM((groups, 1, 128), jnp.int32),
            pltpu.SMEM((groups, 1, 128), jnp.int32),
            pltpu.VMEM((groups, 16, width), bf),
            [pltpu.VMEM((groups, rows // chunks, width), bf)] * chunks,
            pltpu.VMEM((groups, rows, width), bf),
            pltpu.VMEM((depth, width), bf),
            pltpu.VMEM((depth, width), bf),
            pltpu.VMEM((rows_all, width), bf),
            pltpu.VMEM((rows_all, width), bf),
            pltpu.VMEM((depth, data_rows), bf),
            pltpu.VMEM((depth, width), f32),
            pltpu.VMEM((depth, width), f32),
            pltpu.VMEM((rows_all, width), bf),
            pltpu.VMEM((data_rows, width), f32),
            pltpu.VMEM((data_rows, TILE), f32),
            pltpu.VMEM((1, padded), f32),
            pltpu.VMEM((16, width), f32),
            pltpu.VMEM((16, width), f32),
            pltpu.VMEM((16, width), f32),
            pltpu.VMEM((16, width), f32),
            pltpu.VMEM((3, 8, padded), f32),
            pltpu.VMEM((3, hids, 8, padded), f32),
        ] + [dma((groups,))] * 4 + [dma((chunks, groups))] * 8 + [dma((3, hids))] * 2 + [dma((4,))],
        compiler_params=pltpu.CompilerParams(
            collective_id=0, has_side_effects=True, vmem_limit_bytes=56 * 1024 * 1024),
        cost_estimate=pl.CostEstimate(
            flops=10 * data_rows * depth * width, bytes_accessed=8 * depth * width,
            transcendentals=3 * data_rows * width),
    )(ancestors, accepted, particles, noise, data, targets[None])
    return moved, fit[0, :1]


def solution(mesh):
    groups, hids = mesh.shape["dom"], mesh.shape["hid"]
    return jax.shard_map(
        functools.partial(body, groups, hids),
        mesh=mesh,
        in_specs=(P("dom", None, "hid"), P("dom", None, "hid"), P("dom"), P("dom"), P(), P()),
        out_specs=(P("dom", None, "hid"), P("dom")),
        check_vma=False,
    )
```

```python
import functools

import jax
import jax.numpy as jnp
from jax import lax
from jax.experimental import pallas as pl
from jax.experimental.pallas import tpu as pltpu
from jax.sharding import PartitionSpec as P

TEMPER_LEVEL = 0.125
NOISE_INV_VARIANCE = 4.0
STEP_SIZE = 0.4
MESH = pl.DeviceIdType.MESH
TILE = 256
CHUNK = 16
CHUNKS = 2


def kernel(
    groups, hids, chunks,
    anc_ref, acc_ref, part_ref, noise_ref, data_ref, tgt_ref,
    main_out, fit_out,
    anc_all, anc_s, tails, recv, picked, theta0, mass, part_v, noise_v, data_t, mom, pos, moved, hid, resid,
    tgt, tpos, tpos0, tmom, tinv, part_buf, part_all,
    anc_ss, anc_rs, tail_ss, tail_rs, p_ss, p_rs, q_ss, q_rs,
    up_ss, down_ss, side_ss, mass_rs, h_ss, h_rs, loc,
):
    me = lax.axis_index("dom")
    my_hid = lax.axis_index("hid")
    depth, width = theta0.shape
    rows = depth // groups
    piece = rows // chunks
    data_rows = data_ref.shape[0]
    padded = part_buf.shape[-1]
    in_scale = depth ** (-0.5)
    out_scale = (width * hids) ** (-0.5)
    half = groups // 2
    offsets = range(1, groups)
    far, near = list(range(half, groups)), list(range(1, half))
    far_first = [m for pair in zip(far, near) for m in pair] + far[half - 1:]
    near_first = [m for pair in zip(near, far) for m in pair] + far[half - 1:]

    def flip(m):
        t = me
        for bit in range(groups.bit_length() - 1):
            if m >> bit & 1:
                t = t + (1 << bit) - 2 * (1 << bit) * lax.rem(me // (1 << bit), 2)
        return t

    def target(s):
        odd = lax.rem(me // 2 + my_hid, 2)
        first, second = flip(far_first[s]), flip(near_first[s])
        return first + odd * (second - first)

    def wrap(i, n):
        return lax.rem(i, n)

    def block(i, ch):
        return pl.ds(pl.multiple_of(i * rows + ch * piece, piece), piece)

    part_load = pltpu.make_async_copy(part_ref.at[0], part_v, loc.at[1])
    part_load.start()
    noise_copy = pltpu.make_async_copy(noise_ref.at[0], noise_v, loc.at[0])
    noise_copy.start()
    anc_all[me] = jnp.full((1, 128), anc_ref[0], jnp.int32)

    barrier = pltpu.get_barrier_semaphore()
    for k in range(1, groups):
        pl.semaphore_signal(barrier, inc=1, device_id=(wrap(me + k, groups), my_hid), device_id_type=MESH)
    for k in range(1, hids):
        pl.semaphore_signal(barrier, inc=1, device_id=(me, wrap(my_hid + k, hids)), device_id_type=MESH)
    pl.semaphore_wait(barrier, groups - 1 + hids - 1)

    def anc_copy(t, slot):
        return pltpu.make_async_remote_copy(
            anc_all.at[slot], anc_all.at[slot], anc_ss.at[t], anc_rs.at[slot],
            device_id=(t, my_hid), device_id_type=MESH)

    def tail_copy(t, slot):
        return pltpu.make_async_remote_copy(
            tails.at[slot], tails.at[slot], tail_ss.at[t], tail_rs.at[slot],
            device_id=(t, my_hid), device_id_type=MESH)

    def local_rows(ch):
        return pl.ds(ch * piece, piece)

    def part_copy(t, slot, ch):
        return pltpu.make_async_remote_copy(
            part_ref.at[0, block(t, ch)], recv[ch].at[slot], p_ss.at[ch, t], p_rs.at[ch, slot],
            device_id=(t, my_hid), device_id_type=MESH)

    def pick_copy(t, slot, ch):
        return pltpu.make_async_remote_copy(
            picked.at[t, local_rows(ch)], theta0.at[block(slot, ch)], q_ss.at[ch, t], q_rs.at[ch, slot],
            device_id=(t, my_hid), device_id_type=MESH)

    for k in offsets:
        anc_copy(wrap(me + k, groups), me).start()
    for ch in range(chunks):
        for s in range(groups - 1):
            part_copy(target(s), me, ch).start()

    data_t[...] = jnp.transpose(data_ref[...].astype(jnp.float32)).astype(jnp.bfloat16)
    tgt[...] = jnp.zeros_like(tgt)
    tgt[:, 0:data_rows] = tgt_ref[...]
    part_load.wait()
    tails[me] = jnp.zeros((16, width), jnp.bfloat16)
    tails[me, 0:2] = part_v[depth:depth + 2]
    for k in offsets:
        tail_copy(wrap(me + k, groups), me).start()
    for ch in range(chunks):
        recv[ch][me] = part_v[block(me, ch)]
    noise_copy.wait()

    for k in offsets:
        s = wrap(me + groups - k, groups)
        anc_copy(s, s).wait_recv()
    scalars = pltpu.make_async_copy(anc_all, anc_s, loc.at[2])
    scalars.start()
    scalars.wait()

    shrink = groups / (groups + 5.0)
    floor_term = 0.001 * 5.0 / (groups + 5.0)

    def finish(total, square):
        mean = total / groups
        return (shrink * (square / groups - mean * mean) + floor_term).astype(jnp.bfloat16)

    for k in offsets:
        s = wrap(me + groups - k, groups)
        tail_copy(s, s).wait_recv()

    def add_tail(i, carry):
        total, square = carry
        wide = tails[anc_s[i, 0, 0]].astype(jnp.float32)
        return total + wide, square + wide * wide

    zero = jnp.zeros((16, width), jnp.float32)
    tinv[...] = finish(*lax.fori_loop(0, groups, add_tail, (zero, zero))).astype(jnp.float32)
    tpos0[...] = tails[anc_s[me, 0, 0]].astype(jnp.float32)
    tpos[...] = tpos0[...]
    tmom[0:2] = noise_v[depth:depth + 2].astype(jnp.float32) * lax.rsqrt(tinv[0:2])

    place, inner = me // 2, lax.rem(me, 2)

    def mass_copy(t, who, ch, sem):
        return pltpu.make_async_remote_copy(
            mass.at[block(who, ch)], mass.at[block(who, ch)], sem.at[ch, who], mass_rs.at[ch, who],
            device_id=(t, my_hid), device_id_type=MESH)

    def spread(who, ch, up, down):
        @pl.when(lax.rem(my_hid, 2) == 1)
        def _():
            mass_copy(me + 1 - 2 * inner, who, ch, side_ss).start()

        if up:
            @pl.when(place < half - 1)
            def _():
                mass_copy(me + 2, who, ch, up_ss).start()
        if down:
            @pl.when(place > 0)
            def _():
                mass_copy(me - 2, who, ch, down_ss).start()

        @pl.when(lax.rem(my_hid, 2) == 0)
        def _():
            mass_copy(me + 1 - 2 * inner, who, ch, side_ss).start()

    def select(ch):
        for k in offsets:
            s = wrap(me + groups - k, groups)
            part_copy(s, s, ch).wait_recv()

        @pl.loop(0, piece // CHUNK)
        def _(r):
            here = pl.ds(pl.multiple_of(ch * piece + r * CHUNK, CHUNK), CHUNK)

            def add(i, carry):
                total, square = carry
                got = recv[ch][anc_s[i, 0, 0], pl.ds(pl.multiple_of(r * CHUNK, CHUNK), CHUNK)]
                picked[i, here] = got
                wide = got.astype(jnp.float32)
                return total + wide, square + wide * wide

            zero = jnp.zeros((CHUNK, width), jnp.float32)
            carry = (zero, zero)
            if groups <= 8:
                for i in range(groups):
                    carry = add(i, carry)
            else:
                carry = lax.fori_loop(0, groups, add, carry)
            there = pl.ds(pl.multiple_of(me * rows + ch * piece + r * CHUNK, CHUNK), CHUNK)
            mass[there] = finish(*carry)
            theta0[there] = picked[me, here]

        spread(me, ch, True, True)

    def forward_mass(s, ch):
        @pl.when(place >= s)
        def _():
            mass_copy(me, me - 2 * s, ch, up_ss).wait_recv()
            spread(me - 2 * s, ch, True, False)

        @pl.when(place + s < half)
        def _():
            mass_copy(me, me + 2 * s, ch, up_ss).wait_recv()
            spread(me + 2 * s, ch, False, True)

    stages = chunks + half - 1
    pending = []
    quota = -(-chunks * (groups - 1) // stages)
    for stage in range(stages):
        if stage < chunks:
            select(stage)
            pending += [(s, stage) for s in range(groups - 1)]
        for s, ch in pending[:quota]:
            pick_copy(target(s), me, ch).start()
        pending = pending[quota:]
        for s in range(1, half):
            if 0 <= stage - s < chunks:
                forward_mass(s, stage - s)

    for ch in range(chunks):
        for k in offsets:
            s = wrap(me + groups - k, groups)
            pick_copy(s, s, ch).wait_recv()

    def forward(weights, cols, keep_hidden):
        pre = jnp.dot(data_ref[...], weights, preferred_element_type=jnp.float32)
        h = jnp.tanh(pre * in_scale + tpos[0:1, cols])
        if keep_hidden:
            hid[:, cols] = h
        weighted = h * tpos[1:2, cols]
        total = weighted[:, 0:128]
        for c in range(128, TILE, 128):
            total = total + weighted[:, c:c + 128]
        return total

    def tile(c):
        return pl.ds(pl.multiple_of(c * TILE, TILE), TILE)

    none = jnp.zeros((data_rows, 128), jnp.float32)
    tiles = width // TILE

    def outputs(stage, total):
        total = jnp.concatenate([total, jnp.zeros((padded - data_rows, 128), jnp.float32)], axis=0)
        flat = jnp.sum(jnp.transpose(total), axis=0, keepdims=True) * out_scale
        part_buf[stage] = jnp.broadcast_to(flat, (8, padded))

        def copy(t, slot):
            return pltpu.make_async_remote_copy(
                part_buf.at[stage], part_all.at[stage, slot], h_ss.at[stage, t], h_rs.at[stage, slot],
                device_id=(me, t), device_id_type=MESH)

        for k in range(1, hids):
            copy(wrap(my_hid + k, hids), my_hid).start()
        part_all[stage, my_hid] = part_buf[stage]
        for k in range(1, hids):
            s = wrap(my_hid + k, hids)
            copy(s, s).wait_recv()
        for k in range(1, hids):
            copy(wrap(my_hid + k, hids), my_hid).wait_send()
        result = part_all[stage, 0]
        for j in range(1, hids):
            result = result + part_all[stage, j]
        return result[0:1]

    def set_resid(result):
        r = TEMPER_LEVEL * NOISE_INV_VARIANCE * (result - tgt[...])
        column = jnp.transpose(jnp.broadcast_to(r, (128, padded)))[0:data_rows]
        for c in range(0, TILE, 128):
            resid[:, c:c + 128] = column

    keep = acc_ref[0] == 1

    def backward(cols, step):
        h = hid[:, cols]
        b, v = tpos[0:1, cols], tpos[1:2, cols]
        res = resid[...]
        grad_v = jnp.sum(res * h, axis=0, keepdims=True) * out_scale + v
        back = res * (v * out_scale) * (1.0 - h * h)
        grad_b = jnp.sum(back, axis=0, keepdims=True) + b
        grad = jnp.dot(data_t[...], back.astype(jnp.bfloat16), preferred_element_type=jnp.float32) * in_scale
        tm = tmom[0:2, cols] - step * jnp.concatenate([grad_b, grad_v], axis=0)
        tmom[0:2, cols] = tm
        tpos[0:2, cols] = tpos[0:2, cols] + STEP_SIZE * tinv[0:2, cols] * tm
        return grad

    start = lax.fori_loop(
        0, tiles, lambda c, total: total + forward(theta0[:, tile(c)], tile(c), True), none)
    outputs0 = outputs(0, start)
    set_resid(outputs0)

    @pl.loop(0, tiles)
    def _(c):
        cols = tile(c)
        mom[:, cols] = backward(cols, 0.5 * STEP_SIZE) + theta0[:, cols].astype(jnp.float32)

    for ch in range(chunks):
        for q in range(half):
            mass_copy(me, 2 * q + 1 - inner, ch, side_ss).wait_recv()

    def first_move(c, total):
        cols = tile(c)
        inv = mass[:, cols].astype(jnp.float32)
        m = noise_v[0:depth, cols].astype(jnp.float32) * lax.rsqrt(inv) - 0.5 * STEP_SIZE * mom[:, cols]
        w = theta0[:, cols].astype(jnp.float32) + STEP_SIZE * inv * m
        mom[:, cols] = m
        pos[:, cols] = w
        return total + forward(w.astype(jnp.bfloat16), cols, True)

    def last_move(c, total):
        cols = tile(c)
        w = pos[:, cols]
        m = mom[:, cols] - STEP_SIZE * (backward(cols, STEP_SIZE) + w)
        w = w + STEP_SIZE * mass[:, cols].astype(jnp.float32) * m
        moved[0:depth, cols] = jnp.where(keep, w, theta0[:, cols].astype(jnp.float32)).astype(jnp.bfloat16)
        return total + forward(w.astype(jnp.bfloat16), cols, False)

    set_resid(outputs(1, lax.fori_loop(0, tiles, first_move, none)))
    last = lax.fori_loop(0, tiles, last_move, none)
    moved[depth:depth + 2] = jnp.where(keep, tpos[0:2], tpos0[0:2]).astype(jnp.bfloat16)
    result_copy = pltpu.make_async_copy(moved, main_out.at[0], loc.at[3])
    result_copy.start()
    outputs2 = outputs(2, last)
    miss = tgt[...] - jnp.where(keep, outputs2, outputs0)
    fit_out[...] = jnp.broadcast_to(jnp.sum(miss * miss, axis=1, keepdims=True) / data_rows, fit_out.shape)

    result_copy.wait()
    for k in offsets:
        t = wrap(me + k, groups)
        anc_copy(t, me).wait_send()
        tail_copy(t, me).wait_send()
    for ch in range(chunks):
        for k in offsets:
            t = wrap(me + k, groups)
            part_copy(t, me, ch).wait_send()
            pick_copy(t, me, ch).wait_send()
        for q in range(half):
            who = 2 * q + inner
            mass_copy(me, who, ch, side_ss).wait_send()

            @pl.when((q <= place) & (place < half - 1))
            def _():
                mass_copy(me, who, ch, up_ss).wait_send()

            @pl.when((q >= place) & (place > 0))
            def _():
                mass_copy(me, who, ch, down_ss).wait_send()


def copy_kernel(parts, in_ref, out_ref, sems):
    def copy(c):
        cols = pl.ds(c * TILE, TILE)
        return pltpu.make_async_copy(in_ref.at[0, :, cols], out_ref.at[0, :, cols], sems.at[c])

    for c in range(parts):
        copy(c).start()
    for c in range(parts):
        copy(c).wait()


def body(groups, hids, particles, noise, ancestors, accepted, data, targets):
    _, rows_all, width = particles.shape
    depth = rows_all - 2
    rows = depth // groups
    chunks = min(CHUNKS, rows // CHUNK)
    data_rows = data.shape[0]
    padded = -(-data_rows // 128) * 128
    bf, f32 = jnp.bfloat16, jnp.float32
    vm = pl.BlockSpec(memory_space=pltpu.VMEM)
    sm = pl.BlockSpec(memory_space=pltpu.SMEM)
    anywhere = pl.BlockSpec(memory_space=pl.ANY)
    dma = pltpu.SemaphoreType.DMA
    moved, fit = pl.pallas_call(
        functools.partial(kernel, groups, hids, chunks),
        out_shape=(
            jax.ShapeDtypeStruct((1, rows_all, width), bf),
            jax.ShapeDtypeStruct((1, 128), f32),
        ),
        in_specs=[sm, sm, anywhere, anywhere, vm, vm],
        out_specs=(anywhere, vm),
        scratch_shapes=[
            pltpu.VMEM((groups, 1, 128), jnp.int32),
            pltpu.SMEM((groups, 1, 128), jnp.int32),
            pltpu.VMEM((groups, 16, width), bf),
            [pltpu.VMEM((groups, rows // chunks, width), bf)] * chunks,
            pltpu.VMEM((groups, rows, width), bf),
            pltpu.VMEM((depth, width), bf),
            pltpu.VMEM((depth, width), bf),
            pltpu.VMEM((rows_all, width), bf),
            pltpu.VMEM((rows_all, width), bf),
            pltpu.VMEM((depth, data_rows), bf),
            pltpu.VMEM((depth, width), f32),
            pltpu.VMEM((depth, width), f32),
            pltpu.VMEM((rows_all, width), bf),
            pltpu.VMEM((data_rows, width), f32),
            pltpu.VMEM((data_rows, TILE), f32),
            pltpu.VMEM((1, padded), f32),
            pltpu.VMEM((16, width), f32),
            pltpu.VMEM((16, width), f32),
            pltpu.VMEM((16, width), f32),
            pltpu.VMEM((16, width), f32),
            pltpu.VMEM((3, 8, padded), f32),
            pltpu.VMEM((3, hids, 8, padded), f32),
        ] + [dma((groups,))] * 4 + [dma((chunks, groups))] * 8 + [dma((3, hids))] * 2 + [dma((4,))],
        compiler_params=pltpu.CompilerParams(
            collective_id=0, has_side_effects=True, vmem_limit_bytes=56 * 1024 * 1024),
        cost_estimate=pl.CostEstimate(
            flops=10 * data_rows * depth * width, bytes_accessed=8 * depth * width,
            transcendentals=3 * data_rows * width),
    )(ancestors, accepted, particles, noise, data, targets[None])
    parts = width // TILE
    moved = pl.pallas_call(
        functools.partial(copy_kernel, parts),
        out_shape=jax.ShapeDtypeStruct(moved.shape, bf),
        in_specs=[anywhere],
        out_specs=anywhere,
        scratch_shapes=[dma((parts,))],
        cost_estimate=pl.CostEstimate(
            flops=0, bytes_accessed=4 * rows_all * width, transcendentals=0),
    )(moved)
    return moved, fit[0, :1]


def solution(mesh):
    groups, hids = mesh.shape["dom"], mesh.shape["hid"]
    return jax.shard_map(
        functools.partial(body, groups, hids),
        mesh=mesh,
        in_specs=(P("dom", None, "hid"), P("dom", None, "hid"), P("dom"), P("dom"), P(), P()),
        out_specs=(P("dom", None, "hid"), P("dom")),
        check_vma=False,
    )
```

```python
import functools

import jax
import jax.numpy as jnp
from jax import lax
from jax.experimental import pallas as pl
from jax.experimental.pallas import tpu as pltpu
from jax.sharding import PartitionSpec as P

TEMPER_LEVEL = 0.125
NOISE_INV_VARIANCE = 4.0
STEP_SIZE = 0.4
MESH = pl.DeviceIdType.MESH
TILE = 256
CHUNK = 16
CHUNKS = 2


def kernel(
    groups, hids, chunks,
    anc_ref, acc_ref, part_ref, noise_ref, data_ref, tgt_ref,
    main_out, fit_out,
    anc_all, anc_s, tails, recv, picked, theta0, mass, part_v, noise_v, data_t, mom, pos, moved, hid, resid,
    tgt, tpos, tpos0, tmom, tinv, part_buf, part_all,
    anc_ss, anc_rs, tail_ss, tail_rs, p_ss, p_rs, q_ss, q_rs,
    up_ss, down_ss, side_ss, mass_rs, h_ss, h_rs, loc,
):
    me = lax.axis_index("dom")
    my_hid = lax.axis_index("hid")
    depth, width = theta0.shape
    rows = depth // groups
    piece = rows // chunks
    data_rows = data_ref.shape[0]
    padded = part_buf.shape[-1]
    in_scale = depth ** (-0.5)
    out_scale = (width * hids) ** (-0.5)
    half = groups // 2
    offsets = range(1, groups)
    far, near = list(range(half, groups)), list(range(1, half))
    far_first = [m for pair in zip(far, near) for m in pair] + far[half - 1:]
    near_first = [m for pair in zip(near, far) for m in pair] + far[half - 1:]

    def flip(m):
        t = me
        for bit in range(groups.bit_length() - 1):
            if m >> bit & 1:
                t = t + (1 << bit) - 2 * (1 << bit) * lax.rem(me // (1 << bit), 2)
        return t

    def target(s):
        odd = lax.rem(me // 2 + my_hid, 2)
        first, second = flip(far_first[s]), flip(near_first[s])
        return first + odd * (second - first)

    def wrap(i, n):
        return lax.rem(i, n)

    def block(i, ch):
        return pl.ds(pl.multiple_of(i * rows + ch * piece, piece), piece)

    part_load = pltpu.make_async_copy(part_ref.at[0], part_v, loc.at[1])
    part_load.start()
    noise_copy = pltpu.make_async_copy(noise_ref.at[0], noise_v, loc.at[0])
    noise_copy.start()
    anc_all[me] = jnp.full((1, 128), anc_ref[0], jnp.int32)

    barrier = pltpu.get_barrier_semaphore()
    for k in range(1, groups):
        pl.semaphore_signal(barrier, inc=1, device_id=(wrap(me + k, groups), my_hid), device_id_type=MESH)
    for k in range(1, hids):
        pl.semaphore_signal(barrier, inc=1, device_id=(me, wrap(my_hid + k, hids)), device_id_type=MESH)
    pl.semaphore_wait(barrier, groups - 1 + hids - 1)

    def anc_copy(t, slot):
        return pltpu.make_async_remote_copy(
            anc_all.at[slot], anc_all.at[slot], anc_ss.at[t], anc_rs.at[slot],
            device_id=(t, my_hid), device_id_type=MESH)

    def tail_copy(t, slot):
        return pltpu.make_async_remote_copy(
            tails.at[slot], tails.at[slot], tail_ss.at[t], tail_rs.at[slot],
            device_id=(t, my_hid), device_id_type=MESH)

    def local_rows(ch):
        return pl.ds(ch * piece, piece)

    def part_copy(t, slot, ch):
        return pltpu.make_async_remote_copy(
            part_v.at[block(t, ch)], recv[ch].at[slot], p_ss.at[ch, t], p_rs.at[ch, slot],
            device_id=(t, my_hid), device_id_type=MESH)

    def pick_copy(t, slot, ch):
        return pltpu.make_async_remote_copy(
            picked.at[t, local_rows(ch)], theta0.at[block(slot, ch)], q_ss.at[ch, t], q_rs.at[ch, slot],
            device_id=(t, my_hid), device_id_type=MESH)

    for k in offsets:
        anc_copy(wrap(me + k, groups), me).start()
    part_load.wait()
    for ch in range(chunks):
        for s in range(groups - 1):
            part_copy(target(s), me, ch).start()

    data_t[...] = jnp.transpose(data_ref[...].astype(jnp.float32)).astype(jnp.bfloat16)
    tgt[...] = jnp.zeros_like(tgt)
    tgt[:, 0:data_rows] = tgt_ref[...]
    tails[me] = jnp.zeros((16, width), jnp.bfloat16)
    tails[me, 0:2] = part_v[depth:depth + 2]
    for k in offsets:
        tail_copy(wrap(me + k, groups), me).start()
    for ch in range(chunks):
        recv[ch][me] = part_v[block(me, ch)]
    noise_copy.wait()

    for k in offsets:
        s = wrap(me + groups - k, groups)
        anc_copy(s, s).wait_recv()
    scalars = pltpu.make_async_copy(anc_all, anc_s, loc.at[2])
    scalars.start()
    scalars.wait()

    shrink = groups / (groups + 5.0)
    floor_term = 0.001 * 5.0 / (groups + 5.0)

    def finish(total, square):
        mean = total / groups
        return (shrink * (square / groups - mean * mean) + floor_term).astype(jnp.bfloat16)

    for k in offsets:
        s = wrap(me + groups - k, groups)
        tail_copy(s, s).wait_recv()

    def add_tail(i, carry):
        total, square = carry
        wide = tails[anc_s[i, 0, 0]].astype(jnp.float32)
        return total + wide, square + wide * wide

    zero = jnp.zeros((16, width), jnp.float32)
    tinv[...] = finish(*lax.fori_loop(0, groups, add_tail, (zero, zero))).astype(jnp.float32)
    tpos0[...] = tails[anc_s[me, 0, 0]].astype(jnp.float32)
    tpos[...] = tpos0[...]
    tmom[0:2] = noise_v[depth:depth + 2].astype(jnp.float32) * lax.rsqrt(tinv[0:2])

    place, inner = me // 2, lax.rem(me, 2)

    def mass_copy(t, who, ch, sem):
        return pltpu.make_async_remote_copy(
            mass.at[block(who, ch)], mass.at[block(who, ch)], sem.at[ch, who], mass_rs.at[ch, who],
            device_id=(t, my_hid), device_id_type=MESH)

    def spread(who, ch, up, down):
        @pl.when(lax.rem(my_hid, 2) == 1)
        def _():
            mass_copy(me + 1 - 2 * inner, who, ch, side_ss).start()

        if up:
            @pl.when(place < half - 1)
            def _():
                mass_copy(me + 2, who, ch, up_ss).start()
        if down:
            @pl.when(place > 0)
            def _():
                mass_copy(me - 2, who, ch, down_ss).start()

        @pl.when(lax.rem(my_hid, 2) == 0)
        def _():
            mass_copy(me + 1 - 2 * inner, who, ch, side_ss).start()

    def select(ch):
        for k in offsets:
            s = wrap(me + groups - k, groups)
            part_copy(s, s, ch).wait_recv()

        @pl.loop(0, piece // CHUNK)
        def _(r):
            here = pl.ds(pl.multiple_of(ch * piece + r * CHUNK, CHUNK), CHUNK)

            def add(i, carry):
                total, square = carry
                got = recv[ch][anc_s[i, 0, 0], pl.ds(pl.multiple_of(r * CHUNK, CHUNK), CHUNK)]
                picked[i, here] = got
                wide = got.astype(jnp.float32)
                return total + wide, square + wide * wide

            zero = jnp.zeros((CHUNK, width), jnp.float32)
            carry = (zero, zero)
            if groups <= 8:
                for i in range(groups):
                    carry = add(i, carry)
            else:
                carry = lax.fori_loop(0, groups, add, carry)
            there = pl.ds(pl.multiple_of(me * rows + ch * piece + r * CHUNK, CHUNK), CHUNK)
            mass[there] = finish(*carry)
            theta0[there] = picked[me, here]

        spread(me, ch, True, True)

    def forward_mass(s, ch):
        @pl.when(place >= s)
        def _():
            mass_copy(me, me - 2 * s, ch, up_ss).wait_recv()
            spread(me - 2 * s, ch, True, False)

        @pl.when(place + s < half)
        def _():
            mass_copy(me, me + 2 * s, ch, up_ss).wait_recv()
            spread(me + 2 * s, ch, False, True)

    stages = chunks + half - 1
    pending = []
    quota = -(-chunks * (groups - 1) // stages)
    for stage in range(stages):
        if stage < chunks:
            select(stage)
            pending += [(s, stage) for s in range(groups - 1)]
        for s, ch in pending[:quota]:
            pick_copy(target(s), me, ch).start()
        pending = pending[quota:]
        for s in range(1, half):
            if 0 <= stage - s < chunks:
                forward_mass(s, stage - s)

    for ch in range(chunks):
        for k in offsets:
            s = wrap(me + groups - k, groups)
            pick_copy(s, s, ch).wait_recv()

    def forward(weights, cols, keep_hidden):
        pre = jnp.dot(data_ref[...], weights, preferred_element_type=jnp.float32)
        h = jnp.tanh(pre * in_scale + tpos[0:1, cols])
        if keep_hidden:
            hid[:, cols] = h
        weighted = h * tpos[1:2, cols]
        total = weighted[:, 0:128]
        for c in range(128, TILE, 128):
            total = total + weighted[:, c:c + 128]
        return total

    def tile(c):
        return pl.ds(pl.multiple_of(c * TILE, TILE), TILE)

    none = jnp.zeros((data_rows, 128), jnp.float32)
    tiles = width // TILE

    def outputs(stage, total):
        total = jnp.concatenate([total, jnp.zeros((padded - data_rows, 128), jnp.float32)], axis=0)
        flat = jnp.sum(jnp.transpose(total), axis=0, keepdims=True) * out_scale
        part_buf[stage] = jnp.broadcast_to(flat, (8, padded))

        def copy(t, slot):
            return pltpu.make_async_remote_copy(
                part_buf.at[stage], part_all.at[stage, slot], h_ss.at[stage, t], h_rs.at[stage, slot],
                device_id=(me, t), device_id_type=MESH)

        for k in range(1, hids):
            copy(wrap(my_hid + k, hids), my_hid).start()
        part_all[stage, my_hid] = part_buf[stage]
        for k in range(1, hids):
            s = wrap(my_hid + k, hids)
            copy(s, s).wait_recv()
        for k in range(1, hids):
            copy(wrap(my_hid + k, hids), my_hid).wait_send()
        result = part_all[stage, 0]
        for j in range(1, hids):
            result = result + part_all[stage, j]
        return result[0:1]

    def set_resid(result):
        r = TEMPER_LEVEL * NOISE_INV_VARIANCE * (result - tgt[...])
        column = jnp.transpose(jnp.broadcast_to(r, (128, padded)))[0:data_rows]
        for c in range(0, TILE, 128):
            resid[:, c:c + 128] = column

    keep = acc_ref[0] == 1

    def backward(cols, step):
        h = hid[:, cols]
        b, v = tpos[0:1, cols], tpos[1:2, cols]
        res = resid[...]
        grad_v = jnp.sum(res * h, axis=0, keepdims=True) * out_scale + v
        back = res * (v * out_scale) * (1.0 - h * h)
        grad_b = jnp.sum(back, axis=0, keepdims=True) + b
        grad = jnp.dot(data_t[...], back.astype(jnp.bfloat16), preferred_element_type=jnp.float32) * in_scale
        tm = tmom[0:2, cols] - step * jnp.concatenate([grad_b, grad_v], axis=0)
        tmom[0:2, cols] = tm
        tpos[0:2, cols] = tpos[0:2, cols] + STEP_SIZE * tinv[0:2, cols] * tm
        return grad

    start = lax.fori_loop(
        0, tiles, lambda c, total: total + forward(theta0[:, tile(c)], tile(c), True), none)
    outputs0 = outputs(0, start)
    set_resid(outputs0)

    @pl.loop(0, tiles)
    def _(c):
        cols = tile(c)
        mom[:, cols] = backward(cols, 0.5 * STEP_SIZE) + theta0[:, cols].astype(jnp.float32)

    for ch in range(chunks):
        for q in range(half):
            mass_copy(me, 2 * q + 1 - inner, ch, side_ss).wait_recv()

    def first_move(c, total):
        cols = tile(c)
        inv = mass[:, cols].astype(jnp.float32)
        m = noise_v[0:depth, cols].astype(jnp.float32) * lax.rsqrt(inv) - 0.5 * STEP_SIZE * mom[:, cols]
        w = theta0[:, cols].astype(jnp.float32) + STEP_SIZE * inv * m
        mom[:, cols] = m
        pos[:, cols] = w
        return total + forward(w.astype(jnp.bfloat16), cols, True)

    def last_move(c, total):
        cols = tile(c)
        w = pos[:, cols]
        m = mom[:, cols] - STEP_SIZE * (backward(cols, STEP_SIZE) + w)
        w = w + STEP_SIZE * mass[:, cols].astype(jnp.float32) * m
        moved[0:depth, cols] = jnp.where(keep, w, theta0[:, cols].astype(jnp.float32)).astype(jnp.bfloat16)
        return total + forward(w.astype(jnp.bfloat16), cols, False)

    set_resid(outputs(1, lax.fori_loop(0, tiles, first_move, none)))
    last = lax.fori_loop(0, tiles, last_move, none)
    moved[depth:depth + 2] = jnp.where(keep, tpos[0:2], tpos0[0:2]).astype(jnp.bfloat16)
    result_copy = pltpu.make_async_copy(moved, main_out.at[0], loc.at[3])
    result_copy.start()
    outputs2 = outputs(2, last)
    miss = tgt[...] - jnp.where(keep, outputs2, outputs0)
    fit_out[...] = jnp.broadcast_to(jnp.sum(miss * miss, axis=1, keepdims=True) / data_rows, fit_out.shape)

    result_copy.wait()
    for k in offsets:
        t = wrap(me + k, groups)
        anc_copy(t, me).wait_send()
        tail_copy(t, me).wait_send()
    for ch in range(chunks):
        for k in offsets:
            t = wrap(me + k, groups)
            part_copy(t, me, ch).wait_send()
            pick_copy(t, me, ch).wait_send()
        for q in range(half):
            who = 2 * q + inner
            mass_copy(me, who, ch, side_ss).wait_send()

            @pl.when((q <= place) & (place < half - 1))
            def _():
                mass_copy(me, who, ch, up_ss).wait_send()

            @pl.when((q >= place) & (place > 0))
            def _():
                mass_copy(me, who, ch, down_ss).wait_send()


def body(groups, hids, particles, noise, ancestors, accepted, data, targets):
    _, rows_all, width = particles.shape
    depth = rows_all - 2
    rows = depth // groups
    chunks = min(CHUNKS, rows // CHUNK)
    data_rows = data.shape[0]
    padded = -(-data_rows // 128) * 128
    bf, f32 = jnp.bfloat16, jnp.float32
    vm = pl.BlockSpec(memory_space=pltpu.VMEM)
    sm = pl.BlockSpec(memory_space=pltpu.SMEM)
    anywhere = pl.BlockSpec(memory_space=pl.ANY)
    dma = pltpu.SemaphoreType.DMA
    moved, fit = pl.pallas_call(
        functools.partial(kernel, groups, hids, chunks),
        out_shape=(
            jax.ShapeDtypeStruct((1, rows_all, width), bf),
            jax.ShapeDtypeStruct((1, 128), f32),
        ),
        in_specs=[sm, sm, anywhere, anywhere, vm, vm],
        out_specs=(anywhere, vm),
        scratch_shapes=[
            pltpu.VMEM((groups, 1, 128), jnp.int32),
            pltpu.SMEM((groups, 1, 128), jnp.int32),
            pltpu.VMEM((groups, 16, width), bf),
            [pltpu.VMEM((groups, rows // chunks, width), bf)] * chunks,
            pltpu.VMEM((groups, rows, width), bf),
            pltpu.VMEM((depth, width), bf),
            pltpu.VMEM((depth, width), bf),
            pltpu.VMEM((rows_all, width), bf),
            pltpu.VMEM((rows_all, width), bf),
            pltpu.VMEM((depth, data_rows), bf),
            pltpu.VMEM((depth, width), f32),
            pltpu.VMEM((depth, width), f32),
            pltpu.VMEM((rows_all, width), bf),
            pltpu.VMEM((data_rows, width), f32),
            pltpu.VMEM((data_rows, TILE), f32),
            pltpu.VMEM((1, padded), f32),
            pltpu.VMEM((16, width), f32),
            pltpu.VMEM((16, width), f32),
            pltpu.VMEM((16, width), f32),
            pltpu.VMEM((16, width), f32),
            pltpu.VMEM((3, 8, padded), f32),
            pltpu.VMEM((3, hids, 8, padded), f32),
        ] + [dma((groups,))] * 4 + [dma((chunks, groups))] * 8 + [dma((3, hids))] * 2 + [dma((4,))],
        compiler_params=pltpu.CompilerParams(
            collective_id=0, has_side_effects=True, vmem_limit_bytes=56 * 1024 * 1024),
        cost_estimate=pl.CostEstimate(
            flops=10 * data_rows * depth * width, bytes_accessed=8 * depth * width,
            transcendentals=3 * data_rows * width),
    )(ancestors, accepted, particles, noise, data, targets[None])
    return moved, fit[0, :1]


def solution(mesh):
    groups, hids = mesh.shape["dom"], mesh.shape["hid"]
    return jax.shard_map(
        functools.partial(body, groups, hids),
        mesh=mesh,
        in_specs=(P("dom", None, "hid"), P("dom", None, "hid"), P("dom"), P("dom"), P(), P()),
        out_specs=(P("dom", None, "hid"), P("dom")),
        check_vma=False,
    )
```

```python
import functools

import jax
import jax.numpy as jnp
from jax import lax
from jax.experimental import pallas as pl
from jax.experimental.pallas import tpu as pltpu
from jax.sharding import PartitionSpec as P

TEMPER_LEVEL = 0.125
NOISE_INV_VARIANCE = 4.0
STEP_SIZE = 0.4
MESH = pl.DeviceIdType.MESH
TILE = 256
CHUNK = 16
CHUNKS = 4


def kernel(
    groups, hids, chunks,
    anc_ref, acc_ref, part_ref, noise_ref, data_ref, tgt_ref,
    main_out, fit_out,
    anc_all, anc_s, tails, recv, picked, theta0, mass, part_v, noise_v, data_t, mom, pos, moved, hid, resid,
    tgt, tpos, tpos0, tmom, tinv, part_buf, part_all,
    anc_ss, anc_rs, tail_ss, tail_rs, p_ss, p_rs, q_ss, q_rs,
    up_ss, down_ss, side_ss, mass_rs, h_ss, h_rs, loc,
):
    me = lax.axis_index("dom")
    my_hid = lax.axis_index("hid")
    depth, width = theta0.shape
    rows = depth // groups
    piece = rows // chunks
    data_rows = data_ref.shape[0]
    padded = part_buf.shape[-1]
    in_scale = depth ** (-0.5)
    out_scale = (width * hids) ** (-0.5)
    half = groups // 2
    offsets = range(1, groups)
    far, near = list(range(half, groups)), list(range(1, half))
    far_first = [m for pair in zip(far, near) for m in pair] + far[half - 1:]
    near_first = [m for pair in zip(near, far) for m in pair] + far[half - 1:]

    def flip(m):
        t = me
        for bit in range(groups.bit_length() - 1):
            if m >> bit & 1:
                t = t + (1 << bit) - 2 * (1 << bit) * lax.rem(me // (1 << bit), 2)
        return t

    def target(s):
        odd = lax.rem(me // 2 + my_hid, 2)
        first, second = flip(far_first[s]), flip(near_first[s])
        return first + odd * (second - first)

    def wrap(i, n):
        return lax.rem(i, n)

    def block(i, ch):
        return pl.ds(pl.multiple_of(i * rows + ch * piece, piece), piece)

    part_load = pltpu.make_async_copy(part_ref.at[0], part_v, loc.at[1])
    part_load.start()
    noise_copy = pltpu.make_async_copy(noise_ref.at[0], noise_v, loc.at[0])
    noise_copy.start()
    anc_all[me] = jnp.full((1, 128), anc_ref[0], jnp.int32)

    barrier = pltpu.get_barrier_semaphore()
    for k in range(1, groups):
        pl.semaphore_signal(barrier, inc=1, device_id=(wrap(me + k, groups), my_hid), device_id_type=MESH)
    for k in range(1, hids):
        pl.semaphore_signal(barrier, inc=1, device_id=(me, wrap(my_hid + k, hids)), device_id_type=MESH)
    pl.semaphore_wait(barrier, groups - 1 + hids - 1)

    def anc_copy(t, slot):
        return pltpu.make_async_remote_copy(
            anc_all.at[slot], anc_all.at[slot], anc_ss.at[t], anc_rs.at[slot],
            device_id=(t, my_hid), device_id_type=MESH)

    def tail_copy(t, slot):
        return pltpu.make_async_remote_copy(
            tails.at[slot], tails.at[slot], tail_ss.at[t], tail_rs.at[slot],
            device_id=(t, my_hid), device_id_type=MESH)

    def local_rows(ch):
        return pl.ds(ch * piece, piece)

    def part_copy(t, slot, ch):
        return pltpu.make_async_remote_copy(
            part_v.at[block(t, ch)], recv[ch].at[slot], p_ss.at[ch, t], p_rs.at[ch, slot],
            device_id=(t, my_hid), device_id_type=MESH)

    def pick_copy(t, slot, ch):
        return pltpu.make_async_remote_copy(
            picked.at[t, local_rows(ch)], theta0.at[block(slot, ch)], q_ss.at[ch, t], q_rs.at[ch, slot],
            device_id=(t, my_hid), device_id_type=MESH)

    for k in offsets:
        anc_copy(wrap(me + k, groups), me).start()
    part_load.wait()
    for ch in range(chunks):
        for s in range(groups - 1):
            part_copy(target(s), me, ch).start()

    data_t[...] = jnp.transpose(data_ref[...].astype(jnp.float32)).astype(jnp.bfloat16)
    tgt[...] = jnp.zeros_like(tgt)
    tgt[:, 0:data_rows] = tgt_ref[...]
    tails[me] = jnp.zeros((16, width), jnp.bfloat16)
    tails[me, 0:2] = part_v[depth:depth + 2]
    for k in offsets:
        tail_copy(wrap(me + k, groups), me).start()
    for ch in range(chunks):
        recv[ch][me] = part_v[block(me, ch)]
    noise_copy.wait()

    for k in offsets:
        s = wrap(me + groups - k, groups)
        anc_copy(s, s).wait_recv()
    scalars = pltpu.make_async_copy(anc_all, anc_s, loc.at[2])
    scalars.start()
    scalars.wait()

    shrink = groups / (groups + 5.0)
    floor_term = 0.001 * 5.0 / (groups + 5.0)

    def finish(total, square):
        mean = total / groups
        return (shrink * (square / groups - mean * mean) + floor_term).astype(jnp.bfloat16)

    for k in offsets:
        s = wrap(me + groups - k, groups)
        tail_copy(s, s).wait_recv()

    def add_tail(i, carry):
        total, square = carry
        wide = tails[anc_s[i, 0, 0]].astype(jnp.float32)
        return total + wide, square + wide * wide

    zero = jnp.zeros((16, width), jnp.float32)
    tinv[...] = finish(*lax.fori_loop(0, groups, add_tail, (zero, zero))).astype(jnp.float32)
    tpos0[...] = tails[anc_s[me, 0, 0]].astype(jnp.float32)
    tpos[...] = tpos0[...]
    tmom[0:2] = noise_v[depth:depth + 2].astype(jnp.float32) * lax.rsqrt(tinv[0:2])

    place, inner = me // 2, lax.rem(me, 2)

    def mass_copy(t, who, ch, sem):
        return pltpu.make_async_remote_copy(
            mass.at[block(who, ch)], mass.at[block(who, ch)], sem.at[ch, who], mass_rs.at[ch, who],
            device_id=(t, my_hid), device_id_type=MESH)

    def spread(who, ch, up, down):
        @pl.when(lax.rem(my_hid, 2) == 1)
        def _():
            mass_copy(me + 1 - 2 * inner, who, ch, side_ss).start()

        if up:
            @pl.when(place < half - 1)
            def _():
                mass_copy(me + 2, who, ch, up_ss).start()
        if down:
            @pl.when(place > 0)
            def _():
                mass_copy(me - 2, who, ch, down_ss).start()

        @pl.when(lax.rem(my_hid, 2) == 0)
        def _():
            mass_copy(me + 1 - 2 * inner, who, ch, side_ss).start()

    def select(ch):
        for k in offsets:
            s = wrap(me + groups - k, groups)
            part_copy(s, s, ch).wait_recv()

        @pl.loop(0, piece // CHUNK)
        def _(r):
            here = pl.ds(pl.multiple_of(ch * piece + r * CHUNK, CHUNK), CHUNK)

            def add(i, carry):
                total, square = carry
                got = recv[ch][anc_s[i, 0, 0], pl.ds(pl.multiple_of(r * CHUNK, CHUNK), CHUNK)]
                picked[i, here] = got
                wide = got.astype(jnp.float32)
                return total + wide, square + wide * wide

            zero = jnp.zeros((CHUNK, width), jnp.float32)
            carry = (zero, zero)
            if groups <= 8:
                for i in range(groups):
                    carry = add(i, carry)
            else:
                carry = lax.fori_loop(0, groups, add, carry)
            there = pl.ds(pl.multiple_of(me * rows + ch * piece + r * CHUNK, CHUNK), CHUNK)
            mass[there] = finish(*carry)
            theta0[there] = picked[me, here]

        spread(me, ch, True, True)

    def forward_mass(s, ch):
        @pl.when(place >= s)
        def _():
            mass_copy(me, me - 2 * s, ch, up_ss).wait_recv()
            spread(me - 2 * s, ch, True, False)

        @pl.when(place + s < half)
        def _():
            mass_copy(me, me + 2 * s, ch, up_ss).wait_recv()
            spread(me + 2 * s, ch, False, True)

    stages = chunks + half - 1
    pending = []
    quota = -(-chunks * (groups - 1) // stages)
    for stage in range(stages):
        if stage < chunks:
            select(stage)
            pending += [(s, stage) for s in range(groups - 1)]
        for s, ch in pending[:quota]:
            pick_copy(target(s), me, ch).start()
        pending = pending[quota:]
        for s in range(1, half):
            if 0 <= stage - s < chunks:
                forward_mass(s, stage - s)

    for ch in range(chunks):
        for k in offsets:
            s = wrap(me + groups - k, groups)
            pick_copy(s, s, ch).wait_recv()

    def forward(weights, cols, keep_hidden):
        pre = jnp.dot(data_ref[...], weights, preferred_element_type=jnp.float32)
        h = jnp.tanh(pre * in_scale + tpos[0:1, cols])
        if keep_hidden:
            hid[:, cols] = h
        weighted = h * tpos[1:2, cols]
        total = weighted[:, 0:128]
        for c in range(128, TILE, 128):
            total = total + weighted[:, c:c + 128]
        return total

    def tile(c):
        return pl.ds(pl.multiple_of(c * TILE, TILE), TILE)

    none = jnp.zeros((data_rows, 128), jnp.float32)
    tiles = width // TILE

    def outputs(stage, total):
        total = jnp.concatenate([total, jnp.zeros((padded - data_rows, 128), jnp.float32)], axis=0)
        flat = jnp.sum(jnp.transpose(total), axis=0, keepdims=True) * out_scale
        part_buf[stage] = jnp.broadcast_to(flat, (8, padded))

        def copy(t, slot):
            return pltpu.make_async_remote_copy(
                part_buf.at[stage], part_all.at[stage, slot], h_ss.at[stage, t], h_rs.at[stage, slot],
                device_id=(me, t), device_id_type=MESH)

        for k in range(1, hids):
            copy(wrap(my_hid + k, hids), my_hid).start()
        part_all[stage, my_hid] = part_buf[stage]
        for k in range(1, hids):
            s = wrap(my_hid + k, hids)
            copy(s, s).wait_recv()
        for k in range(1, hids):
            copy(wrap(my_hid + k, hids), my_hid).wait_send()
        result = part_all[stage, 0]
        for j in range(1, hids):
            result = result + part_all[stage, j]
        return result[0:1]

    def set_resid(result):
        r = TEMPER_LEVEL * NOISE_INV_VARIANCE * (result - tgt[...])
        column = jnp.transpose(jnp.broadcast_to(r, (128, padded)))[0:data_rows]
        for c in range(0, TILE, 128):
            resid[:, c:c + 128] = column

    keep = acc_ref[0] == 1

    def backward(cols, step):
        h = hid[:, cols]
        b, v = tpos[0:1, cols], tpos[1:2, cols]
        res = resid[...]
        grad_v = jnp.sum(res * h, axis=0, keepdims=True) * out_scale + v
        back = res * (v * out_scale) * (1.0 - h * h)
        grad_b = jnp.sum(back, axis=0, keepdims=True) + b
        grad = jnp.dot(data_t[...], back.astype(jnp.bfloat16), preferred_element_type=jnp.float32) * in_scale
        tm = tmom[0:2, cols] - step * jnp.concatenate([grad_b, grad_v], axis=0)
        tmom[0:2, cols] = tm
        tpos[0:2, cols] = tpos[0:2, cols] + STEP_SIZE * tinv[0:2, cols] * tm
        return grad

    start = lax.fori_loop(
        0, tiles, lambda c, total: total + forward(theta0[:, tile(c)], tile(c), True), none)
    outputs0 = outputs(0, start)
    set_resid(outputs0)

    @pl.loop(0, tiles)
    def _(c):
        cols = tile(c)
        mom[:, cols] = backward(cols, 0.5 * STEP_SIZE) + theta0[:, cols].astype(jnp.float32)

    for ch in range(chunks):
        for q in range(half):
            mass_copy(me, 2 * q + 1 - inner, ch, side_ss).wait_recv()

    def first_move(c, total):
        cols = tile(c)
        inv = mass[:, cols].astype(jnp.float32)
        m = noise_v[0:depth, cols].astype(jnp.float32) * lax.rsqrt(inv) - 0.5 * STEP_SIZE * mom[:, cols]
        w = theta0[:, cols].astype(jnp.float32) + STEP_SIZE * inv * m
        mom[:, cols] = m
        pos[:, cols] = w
        return total + forward(w.astype(jnp.bfloat16), cols, True)

    def last_move(c, total):
        cols = tile(c)
        w = pos[:, cols]
        m = mom[:, cols] - STEP_SIZE * (backward(cols, STEP_SIZE) + w)
        w = w + STEP_SIZE * mass[:, cols].astype(jnp.float32) * m
        moved[0:depth, cols] = jnp.where(keep, w, theta0[:, cols].astype(jnp.float32)).astype(jnp.bfloat16)
        return total + forward(w.astype(jnp.bfloat16), cols, False)

    set_resid(outputs(1, lax.fori_loop(0, tiles, first_move, none)))
    last = lax.fori_loop(0, tiles, last_move, none)
    moved[depth:depth + 2] = jnp.where(keep, tpos[0:2], tpos0[0:2]).astype(jnp.bfloat16)
    result_copy = pltpu.make_async_copy(moved, main_out.at[0], loc.at[3])
    result_copy.start()
    outputs2 = outputs(2, last)
    miss = tgt[...] - jnp.where(keep, outputs2, outputs0)
    fit_out[...] = jnp.broadcast_to(jnp.sum(miss * miss, axis=1, keepdims=True) / data_rows, fit_out.shape)

    result_copy.wait()
    for k in offsets:
        t = wrap(me + k, groups)
        anc_copy(t, me).wait_send()
        tail_copy(t, me).wait_send()
    for ch in range(chunks):
        for k in offsets:
            t = wrap(me + k, groups)
            part_copy(t, me, ch).wait_send()
            pick_copy(t, me, ch).wait_send()
        for q in range(half):
            who = 2 * q + inner
            mass_copy(me, who, ch, side_ss).wait_send()

            @pl.when((q <= place) & (place < half - 1))
            def _():
                mass_copy(me, who, ch, up_ss).wait_send()

            @pl.when((q >= place) & (place > 0))
            def _():
                mass_copy(me, who, ch, down_ss).wait_send()


def body(groups, hids, particles, noise, ancestors, accepted, data, targets):
    _, rows_all, width = particles.shape
    depth = rows_all - 2
    rows = depth // groups
    chunks = min(CHUNKS, rows // CHUNK)
    data_rows = data.shape[0]
    padded = -(-data_rows // 128) * 128
    bf, f32 = jnp.bfloat16, jnp.float32
    vm = pl.BlockSpec(memory_space=pltpu.VMEM)
    sm = pl.BlockSpec(memory_space=pltpu.SMEM)
    anywhere = pl.BlockSpec(memory_space=pl.ANY)
    dma = pltpu.SemaphoreType.DMA
    moved, fit = pl.pallas_call(
        functools.partial(kernel, groups, hids, chunks),
        out_shape=(
            jax.ShapeDtypeStruct((1, rows_all, width), bf),
            jax.ShapeDtypeStruct((1, 128), f32),
        ),
        in_specs=[sm, sm, anywhere, anywhere, vm, vm],
        out_specs=(anywhere, vm),
        scratch_shapes=[
            pltpu.VMEM((groups, 1, 128), jnp.int32),
            pltpu.SMEM((groups, 1, 128), jnp.int32),
            pltpu.VMEM((groups, 16, width), bf),
            [pltpu.VMEM((groups, rows // chunks, width), bf)] * chunks,
            pltpu.VMEM((groups, rows, width), bf),
            pltpu.VMEM((depth, width), bf),
            pltpu.VMEM((depth, width), bf),
            pltpu.VMEM((rows_all, width), bf),
            pltpu.VMEM((rows_all, width), bf),
            pltpu.VMEM((depth, data_rows), bf),
            pltpu.VMEM((depth, width), f32),
            pltpu.VMEM((depth, width), f32),
            pltpu.VMEM((rows_all, width), bf),
            pltpu.VMEM((data_rows, width), f32),
            pltpu.VMEM((data_rows, TILE), f32),
            pltpu.VMEM((1, padded), f32),
            pltpu.VMEM((16, width), f32),
            pltpu.VMEM((16, width), f32),
            pltpu.VMEM((16, width), f32),
            pltpu.VMEM((16, width), f32),
            pltpu.VMEM((3, 8, padded), f32),
            pltpu.VMEM((3, hids, 8, padded), f32),
        ] + [dma((groups,))] * 4 + [dma((chunks, groups))] * 8 + [dma((3, hids))] * 2 + [dma((4,))],
        compiler_params=pltpu.CompilerParams(
            collective_id=0, has_side_effects=True, vmem_limit_bytes=34 * 1024 * 1024),
        cost_estimate=pl.CostEstimate(
            flops=10 * data_rows * depth * width, bytes_accessed=8 * depth * width,
            transcendentals=3 * data_rows * width),
    )(ancestors, accepted, particles, noise, data, targets[None])
    return moved, fit[0, :1]


def solution(mesh):
    groups, hids = mesh.shape["dom"], mesh.shape["hid"]
    return jax.shard_map(
        functools.partial(body, groups, hids),
        mesh=mesh,
        in_specs=(P("dom", None, "hid"), P("dom", None, "hid"), P("dom"), P("dom"), P(), P()),
        out_specs=(P("dom", None, "hid"), P("dom")),
        check_vma=False,
    )
```

```python
import functools

import jax
import jax.numpy as jnp
from jax import lax
from jax.experimental import pallas as pl
from jax.experimental.pallas import tpu as pltpu
from jax.sharding import PartitionSpec as P

TEMPER_LEVEL = 0.125
NOISE_INV_VARIANCE = 4.0
STEP_SIZE = 0.4
MESH = pl.DeviceIdType.MESH
TILE = 256
CHUNK = 16
CHUNKS = 2


def kernel(
    groups, hids, chunks,
    anc_ref, acc_ref, part_ref, noise_ref, data_ref, tgt_ref,
    main_out, fit_out,
    anc_all, anc_s, tails, recv, picked, theta0, mass, part_v, noise_v, data_t, mom, pos, moved, hid, resid,
    tgt, tpos, tpos0, tmom, tinv, part_buf, part_all,
    anc_ss, anc_rs, tail_ss, tail_rs, p_ss, p_rs, q_ss, q_rs,
    up_ss, down_ss, side_ss, mass_rs, h_ss, h_rs, loc,
):
    me = lax.axis_index("dom")
    my_hid = lax.axis_index("hid")
    depth, width = theta0.shape
    rows = depth // groups
    piece = rows // chunks
    data_rows = data_ref.shape[0]
    padded = part_buf.shape[-1]
    in_scale = depth ** (-0.5)
    out_scale = (width * hids) ** (-0.5)
    half = groups // 2
    offsets = range(1, groups)
    far, near = list(range(half, groups)), list(range(1, half))
    far_first = [m for pair in zip(far, near) for m in pair] + far[half - 1:]
    near_first = [m for pair in zip(near, far) for m in pair] + far[half - 1:]

    def flip(m):
        t = me
        for bit in range(groups.bit_length() - 1):
            if m >> bit & 1:
                t = t + (1 << bit) - 2 * (1 << bit) * lax.rem(me // (1 << bit), 2)
        return t

    def target(s):
        odd = lax.rem(me // 2 + my_hid, 2)
        first, second = flip(far_first[s]), flip(near_first[s])
        return first + odd * (second - first)

    def wrap(i, n):
        return lax.rem(i, n)

    def block(i, ch):
        return pl.ds(pl.multiple_of(i * rows + ch * piece, piece), piece)

    part_load = pltpu.make_async_copy(part_ref.at[0], part_v, loc.at[1])
    part_load.start()
    noise_copy = pltpu.make_async_copy(noise_ref.at[0], noise_v, loc.at[0])
    noise_copy.start()
    anc_all[me] = jnp.full((1, 128), anc_ref[0], jnp.int32)

    barrier = pltpu.get_barrier_semaphore()
    for k in range(1, groups):
        pl.semaphore_signal(barrier, inc=1, device_id=(wrap(me + k, groups), my_hid), device_id_type=MESH)
    for k in range(1, hids):
        pl.semaphore_signal(barrier, inc=1, device_id=(me, wrap(my_hid + k, hids)), device_id_type=MESH)
    pl.semaphore_wait(barrier, groups - 1 + hids - 1)

    def anc_copy(t, slot):
        return pltpu.make_async_remote_copy(
            anc_all.at[slot], anc_all.at[slot], anc_ss.at[t], anc_rs.at[slot],
            device_id=(t, my_hid), device_id_type=MESH)

    def tail_copy(t, slot):
        return pltpu.make_async_remote_copy(
            tails.at[slot], tails.at[slot], tail_ss.at[t], tail_rs.at[slot],
            device_id=(t, my_hid), device_id_type=MESH)

    def local_rows(ch):
        return pl.ds(ch * piece, piece)

    def part_copy(t, slot, ch):
        return pltpu.make_async_remote_copy(
            part_v.at[block(t, ch)], recv[ch].at[slot], p_ss.at[ch, t], p_rs.at[ch, slot],
            device_id=(t, my_hid), device_id_type=MESH)

    def pick_copy(t, slot, ch):
        return pltpu.make_async_remote_copy(
            picked.at[t, local_rows(ch)], theta0.at[block(slot, ch)], q_ss.at[ch, t], q_rs.at[ch, slot],
            device_id=(t, my_hid), device_id_type=MESH)

    for k in offsets:
        anc_copy(wrap(me + k, groups), me).start()
    part_load.wait()
    for ch in range(chunks):
        for s in range(groups - 1):
            part_copy(target(s), me, ch).start()

    data_t[...] = jnp.transpose(data_ref[...].astype(jnp.float32)).astype(jnp.bfloat16)
    tgt[...] = jnp.zeros_like(tgt)
    tgt[:, 0:data_rows] = tgt_ref[...]
    tails[me] = jnp.zeros((16, width), jnp.bfloat16)
    tails[me, 0:2] = part_v[depth:depth + 2]
    for k in offsets:
        tail_copy(wrap(me + k, groups), me).start()
    for ch in range(chunks):
        recv[ch][me] = part_v[block(me, ch)]
    noise_copy.wait()

    for k in offsets:
        s = wrap(me + groups - k, groups)
        anc_copy(s, s).wait_recv()
    scalars = pltpu.make_async_copy(anc_all, anc_s, loc.at[2])
    scalars.start()
    scalars.wait()

    shrink = groups / (groups + 5.0)
    floor_term = 0.001 * 5.0 / (groups + 5.0)

    def finish(total, square):
        mean = total / groups
        return (shrink * (square / groups - mean * mean) + floor_term).astype(jnp.bfloat16)

    for k in offsets:
        s = wrap(me + groups - k, groups)
        tail_copy(s, s).wait_recv()

    def add_tail(i, carry):
        total, square = carry
        wide = tails[anc_s[i, 0, 0]].astype(jnp.float32)
        return total + wide, square + wide * wide

    zero = jnp.zeros((16, width), jnp.float32)
    tinv[...] = finish(*lax.fori_loop(0, groups, add_tail, (zero, zero))).astype(jnp.float32)
    tpos0[...] = tails[anc_s[me, 0, 0]].astype(jnp.float32)
    tpos[...] = tpos0[...]
    tmom[0:2] = noise_v[depth:depth + 2].astype(jnp.float32) * lax.rsqrt(tinv[0:2])

    place, inner = me // 2, lax.rem(me, 2)

    def mass_copy(t, who, ch, sem):
        return pltpu.make_async_remote_copy(
            mass.at[block(who, ch)], mass.at[block(who, ch)], sem.at[ch, who], mass_rs.at[ch, who],
            device_id=(t, my_hid), device_id_type=MESH)

    def spread(who, ch, up, down):
        @pl.when(lax.rem(my_hid, 2) == 1)
        def _():
            mass_copy(me + 1 - 2 * inner, who, ch, side_ss).start()

        if up:
            @pl.when(place < half - 1)
            def _():
                mass_copy(me + 2, who, ch, up_ss).start()
        if down:
            @pl.when(place > 0)
            def _():
                mass_copy(me - 2, who, ch, down_ss).start()

        @pl.when(lax.rem(my_hid, 2) == 0)
        def _():
            mass_copy(me + 1 - 2 * inner, who, ch, side_ss).start()

    inward = 1 - 2 * (place // 2)
    is_end = (place == 0) | (place == half - 1)
    step = 2 * inward
    partner = me + 1 - 2 * inner

    def send_own(ch):
        if half != 4:
            spread(me, ch, True, True)
            return

        @pl.when(is_end)
        def _():
            mass_copy(me + step, me, ch, up_ss).start()
            mass_copy(me + 2 * step, me, ch, down_ss).start()

        @pl.when(jnp.logical_not(is_end))
        def _():
            mass_copy(me + step, me, ch, up_ss).start()
            mass_copy(me - step, me, ch, down_ss).start()

        mass_copy(partner, me, ch, side_ss).start()

    def relay(s, ch):
        @pl.when(is_end)
        def _():
            if s == 1:
                mass_copy(me, partner, ch, up_ss).wait_recv()
                mass_copy(me + step, partner, ch, up_ss).start()
            for far_off in ((), (1,), (2, 3))[s - 1]:
                who = me + far_off * step
                mass_copy(me, who, ch, up_ss).wait_recv()
                mass_copy(partner, who, ch, side_ss).start()

        @pl.when(jnp.logical_not(is_end))
        def _():
            if s < 3:
                who = me + s * step
                mass_copy(me, who, ch, up_ss).wait_recv()
                mass_copy(me - step, who, ch, down_ss).start()
                mass_copy(partner, who, ch, side_ss).start()

    def rest_of_mass(ch):
        if half != 4:
            for q in range(half):
                mass_copy(me, 2 * q + 1 - inner, ch, side_ss).wait_recv()
            return

        @pl.when(is_end)
        def _():
            for far_off in (1, 2, 3):
                mass_copy(me, partner + far_off * step, ch, side_ss).wait_recv()

        @pl.when(jnp.logical_not(is_end))
        def _():
            mass_copy(me, me - step, ch, side_ss).wait_recv()
            mass_copy(me, partner - step, ch, side_ss).wait_recv()
            for far_off in (0, 1, 2):
                mass_copy(me, partner + far_off * step, ch, side_ss).wait_recv()

    def mass_sent(ch):
        if half != 4:
            for q in range(half):
                who = 2 * q + inner
                mass_copy(me, who, ch, side_ss).wait_send()

                @pl.when((q <= place) & (place < half - 1))
                def _():
                    mass_copy(me, who, ch, up_ss).wait_send()

                @pl.when((q >= place) & (place > 0))
                def _():
                    mass_copy(me, who, ch, down_ss).wait_send()
            return
        mass_copy(me, me, ch, up_ss).wait_send()
        mass_copy(me, me, ch, down_ss).wait_send()
        mass_copy(me, me, ch, side_ss).wait_send()

        @pl.when(is_end)
        def _():
            mass_copy(me, partner, ch, up_ss).wait_send()
            for far_off in (1, 2, 3):
                mass_copy(me, me + far_off * step, ch, side_ss).wait_send()

        @pl.when(jnp.logical_not(is_end))
        def _():
            for far_off in (1, 2):
                mass_copy(me, me + far_off * step, ch, side_ss).wait_send()
                mass_copy(me, me + far_off * step, ch, down_ss).wait_send()

    def select(ch):
        for k in offsets:
            s = wrap(me + groups - k, groups)
            part_copy(s, s, ch).wait_recv()

        @pl.loop(0, piece // CHUNK)
        def _(r):
            here = pl.ds(pl.multiple_of(ch * piece + r * CHUNK, CHUNK), CHUNK)

            def add(i, carry):
                total, square = carry
                got = recv[ch][anc_s[i, 0, 0], pl.ds(pl.multiple_of(r * CHUNK, CHUNK), CHUNK)]
                picked[i, here] = got
                wide = got.astype(jnp.float32)
                return total + wide, square + wide * wide

            zero = jnp.zeros((CHUNK, width), jnp.float32)
            carry = (zero, zero)
            if groups <= 8:
                for i in range(groups):
                    carry = add(i, carry)
            else:
                carry = lax.fori_loop(0, groups, add, carry)
            there = pl.ds(pl.multiple_of(me * rows + ch * piece + r * CHUNK, CHUNK), CHUNK)
            mass[there] = finish(*carry)
            theta0[there] = picked[me, here]

        send_own(ch)

    def forward_mass(s, ch):
        if half == 4:
            relay(s, ch)
            return

        @pl.when(place >= s)
        def _():
            mass_copy(me, me - 2 * s, ch, up_ss).wait_recv()
            spread(me - 2 * s, ch, True, False)

        @pl.when(place + s < half)
        def _():
            mass_copy(me, me + 2 * s, ch, up_ss).wait_recv()
            spread(me + 2 * s, ch, False, True)

    stages = chunks + half - 1
    pending = []
    quota = -(-chunks * (groups - 1) // stages)
    for stage in range(stages):
        if stage < chunks:
            select(stage)
            pending += [(s, stage) for s in range(groups - 1)]
        for s, ch in pending[:quota]:
            pick_copy(target(s), me, ch).start()
        pending = pending[quota:]
        for s in range(1, half):
            if 0 <= stage - s < chunks:
                forward_mass(s, stage - s)

    for ch in range(chunks):
        for k in offsets:
            s = wrap(me + groups - k, groups)
            pick_copy(s, s, ch).wait_recv()

    def forward(weights, cols, keep_hidden):
        pre = jnp.dot(data_ref[...], weights, preferred_element_type=jnp.float32)
        h = jnp.tanh(pre * in_scale + tpos[0:1, cols])
        if keep_hidden:
            hid[:, cols] = h
        weighted = h * tpos[1:2, cols]
        total = weighted[:, 0:128]
        for c in range(128, TILE, 128):
            total = total + weighted[:, c:c + 128]
        return total

    def tile(c):
        return pl.ds(pl.multiple_of(c * TILE, TILE), TILE)

    none = jnp.zeros((data_rows, 128), jnp.float32)
    tiles = width // TILE

    def outputs(stage, total):
        total = jnp.concatenate([total, jnp.zeros((padded - data_rows, 128), jnp.float32)], axis=0)
        flat = jnp.sum(jnp.transpose(total), axis=0, keepdims=True) * out_scale
        part_buf[stage] = jnp.broadcast_to(flat, (8, padded))

        def copy(t, slot):
            return pltpu.make_async_remote_copy(
                part_buf.at[stage], part_all.at[stage, slot], h_ss.at[stage, t], h_rs.at[stage, slot],
                device_id=(me, t), device_id_type=MESH)

        for k in range(1, hids):
            copy(wrap(my_hid + k, hids), my_hid).start()
        part_all[stage, my_hid] = part_buf[stage]
        for k in range(1, hids):
            s = wrap(my_hid + k, hids)
            copy(s, s).wait_recv()
        for k in range(1, hids):
            copy(wrap(my_hid + k, hids), my_hid).wait_send()
        result = part_all[stage, 0]
        for j in range(1, hids):
            result = result + part_all[stage, j]
        return result[0:1]

    def set_resid(result):
        r = TEMPER_LEVEL * NOISE_INV_VARIANCE * (result - tgt[...])
        column = jnp.transpose(jnp.broadcast_to(r, (128, padded)))[0:data_rows]
        for c in range(0, TILE, 128):
            resid[:, c:c + 128] = column

    keep = acc_ref[0] == 1

    def backward(cols, step):
        h = hid[:, cols]
        b, v = tpos[0:1, cols], tpos[1:2, cols]
        res = resid[...]
        grad_v = jnp.sum(res * h, axis=0, keepdims=True) * out_scale + v
        back = res * (v * out_scale) * (1.0 - h * h)
        grad_b = jnp.sum(back, axis=0, keepdims=True) + b
        grad = jnp.dot(data_t[...], back.astype(jnp.bfloat16), preferred_element_type=jnp.float32) * in_scale
        tm = tmom[0:2, cols] - step * jnp.concatenate([grad_b, grad_v], axis=0)
        tmom[0:2, cols] = tm
        tpos[0:2, cols] = tpos[0:2, cols] + STEP_SIZE * tinv[0:2, cols] * tm
        return grad

    start = lax.fori_loop(
        0, tiles, lambda c, total: total + forward(theta0[:, tile(c)], tile(c), True), none)
    outputs0 = outputs(0, start)
    set_resid(outputs0)

    @pl.loop(0, tiles)
    def _(c):
        cols = tile(c)
        mom[:, cols] = backward(cols, 0.5 * STEP_SIZE) + theta0[:, cols].astype(jnp.float32)

    for ch in range(chunks):
        rest_of_mass(ch)

    def first_move(c, total):
        cols = tile(c)
        inv = mass[:, cols].astype(jnp.float32)
        m = noise_v[0:depth, cols].astype(jnp.float32) * lax.rsqrt(inv) - 0.5 * STEP_SIZE * mom[:, cols]
        w = theta0[:, cols].astype(jnp.float32) + STEP_SIZE * inv * m
        mom[:, cols] = m
        pos[:, cols] = w
        return total + forward(w.astype(jnp.bfloat16), cols, True)

    def last_move(c, total):
        cols = tile(c)
        w = pos[:, cols]
        m = mom[:, cols] - STEP_SIZE * (backward(cols, STEP_SIZE) + w)
        w = w + STEP_SIZE * mass[:, cols].astype(jnp.float32) * m
        moved[0:depth, cols] = jnp.where(keep, w, theta0[:, cols].astype(jnp.float32)).astype(jnp.bfloat16)
        return total + forward(w.astype(jnp.bfloat16), cols, False)

    set_resid(outputs(1, lax.fori_loop(0, tiles, first_move, none)))
    last = lax.fori_loop(0, tiles, last_move, none)
    moved[depth:depth + 2] = jnp.where(keep, tpos[0:2], tpos0[0:2]).astype(jnp.bfloat16)
    result_copy = pltpu.make_async_copy(moved, main_out.at[0], loc.at[3])
    result_copy.start()
    outputs2 = outputs(2, last)
    miss = tgt[...] - jnp.where(keep, outputs2, outputs0)
    fit_out[...] = jnp.broadcast_to(jnp.sum(miss * miss, axis=1, keepdims=True) / data_rows, fit_out.shape)

    result_copy.wait()
    for k in offsets:
        t = wrap(me + k, groups)
        anc_copy(t, me).wait_send()
        tail_copy(t, me).wait_send()
    for ch in range(chunks):
        for k in offsets:
            t = wrap(me + k, groups)
            part_copy(t, me, ch).wait_send()
            pick_copy(t, me, ch).wait_send()
        mass_sent(ch)


def body(groups, hids, particles, noise, ancestors, accepted, data, targets):
    _, rows_all, width = particles.shape
    depth = rows_all - 2
    rows = depth // groups
    chunks = min(CHUNKS, rows // CHUNK)
    data_rows = data.shape[0]
    padded = -(-data_rows // 128) * 128
    bf, f32 = jnp.bfloat16, jnp.float32
    vm = pl.BlockSpec(memory_space=pltpu.VMEM)
    sm = pl.BlockSpec(memory_space=pltpu.SMEM)
    anywhere = pl.BlockSpec(memory_space=pl.ANY)
    dma = pltpu.SemaphoreType.DMA
    moved, fit = pl.pallas_call(
        functools.partial(kernel, groups, hids, chunks),
        out_shape=(
            jax.ShapeDtypeStruct((1, rows_all, width), bf),
            jax.ShapeDtypeStruct((1, 128), f32),
        ),
        in_specs=[sm, sm, anywhere, anywhere, vm, vm],
        out_specs=(anywhere, vm),
        scratch_shapes=[
            pltpu.VMEM((groups, 1, 128), jnp.int32),
            pltpu.SMEM((groups, 1, 128), jnp.int32),
            pltpu.VMEM((groups, 16, width), bf),
            [pltpu.VMEM((groups, rows // chunks, width), bf)] * chunks,
            pltpu.VMEM((groups, rows, width), bf),
            pltpu.VMEM((depth, width), bf),
            pltpu.VMEM((depth, width), bf),
            pltpu.VMEM((rows_all, width), bf),
            pltpu.VMEM((rows_all, width), bf),
            pltpu.VMEM((depth, data_rows), bf),
            pltpu.VMEM((depth, width), f32),
            pltpu.VMEM((depth, width), f32),
            pltpu.VMEM((rows_all, width), bf),
            pltpu.VMEM((data_rows, width), f32),
            pltpu.VMEM((data_rows, TILE), f32),
            pltpu.VMEM((1, padded), f32),
            pltpu.VMEM((16, width), f32),
            pltpu.VMEM((16, width), f32),
            pltpu.VMEM((16, width), f32),
            pltpu.VMEM((16, width), f32),
            pltpu.VMEM((3, 8, padded), f32),
            pltpu.VMEM((3, hids, 8, padded), f32),
        ] + [dma((groups,))] * 4 + [dma((chunks, groups))] * 8 + [dma((3, hids))] * 2 + [dma((4,))],
        compiler_params=pltpu.CompilerParams(
            collective_id=0, has_side_effects=True, vmem_limit_bytes=56 * 1024 * 1024),
        cost_estimate=pl.CostEstimate(
            flops=10 * data_rows * depth * width, bytes_accessed=8 * depth * width,
            transcendentals=3 * data_rows * width),
    )(ancestors, accepted, particles, noise, data, targets[None])
    return moved, fit[0, :1]


def solution(mesh):
    groups, hids = mesh.shape["dom"], mesh.shape["hid"]
    return jax.shard_map(
        functools.partial(body, groups, hids),
        mesh=mesh,
        in_specs=(P("dom", None, "hid"), P("dom", None, "hid"), P("dom"), P("dom"), P(), P()),
        out_specs=(P("dom", None, "hid"), P("dom")),
        check_vma=False,
    )
```

```python
import functools

import jax
import jax.numpy as jnp
from jax import lax
from jax.experimental import pallas as pl
from jax.experimental.pallas import tpu as pltpu
from jax.sharding import PartitionSpec as P

TEMPER_LEVEL = 0.125
NOISE_INV_VARIANCE = 4.0
STEP_SIZE = 0.4
MESH = pl.DeviceIdType.MESH
TILE = 256
CHUNK = 16
CHUNKS = 2


def kernel(
    groups, hids, chunks,
    anc_ref, acc_ref, part_ref, noise_ref, data_ref, tgt_ref,
    main_out, fit_out,
    anc_all, anc_s, tails, recv, picked, theta0, mass, part_v, noise_v, data_t, mom, pos, moved, hid, resid,
    tgt, tpos, tpos0, tmom, tinv, part_buf, part_all,
    anc_ss, anc_rs, tail_ss, tail_rs, p_ss, p_rs, q_ss, q_rs,
    up_ss, down_ss, side_ss, mass_rs, h_ss, h_rs, loc,
):
    me = lax.axis_index("dom")
    my_hid = lax.axis_index("hid")
    depth, width = theta0.shape
    rows = depth // groups
    piece = rows // chunks
    data_rows = data_ref.shape[0]
    padded = part_buf.shape[-1]
    in_scale = depth ** (-0.5)
    out_scale = (width * hids) ** (-0.5)
    half = groups // 2
    offsets = range(1, groups)
    far, near = list(range(half, groups)), list(range(1, half))
    far_first = [m for pair in zip(far, near) for m in pair] + far[half - 1:]
    near_first = [m for pair in zip(near, far) for m in pair] + far[half - 1:]

    def flip(m):
        t = me
        for bit in range(groups.bit_length() - 1):
            if m >> bit & 1:
                t = t + (1 << bit) - 2 * (1 << bit) * lax.rem(me // (1 << bit), 2)
        return t

    def target(s):
        odd = lax.rem(me // 2 + my_hid, 2)
        first, second = flip(far_first[s]), flip(near_first[s])
        return first + odd * (second - first)

    def wrap(i, n):
        return lax.rem(i, n)

    def block(i, ch):
        return pl.ds(pl.multiple_of(i * rows + ch * piece, piece), piece)

    part_load = pltpu.make_async_copy(part_ref.at[0], part_v, loc.at[1])
    part_load.start()
    noise_copy = pltpu.make_async_copy(noise_ref.at[0], noise_v, loc.at[0])
    noise_copy.start()
    anc_all[me] = jnp.full((1, 128), anc_ref[0], jnp.int32)

    barrier = pltpu.get_barrier_semaphore()
    for k in range(1, groups):
        pl.semaphore_signal(barrier, inc=1, device_id=(wrap(me + k, groups), my_hid), device_id_type=MESH)
    for k in range(1, hids):
        pl.semaphore_signal(barrier, inc=1, device_id=(me, wrap(my_hid + k, hids)), device_id_type=MESH)
    pl.semaphore_wait(barrier, groups - 1 + hids - 1)

    def anc_copy(t, slot):
        return pltpu.make_async_remote_copy(
            anc_all.at[slot], anc_all.at[slot], anc_ss.at[t], anc_rs.at[slot],
            device_id=(t, my_hid), device_id_type=MESH)

    def tail_copy(t, slot):
        return pltpu.make_async_remote_copy(
            tails.at[slot], tails.at[slot], tail_ss.at[t], tail_rs.at[slot],
            device_id=(t, my_hid), device_id_type=MESH)

    def local_rows(ch):
        return pl.ds(ch * piece, piece)

    def part_copy(t, slot, ch):
        return pltpu.make_async_remote_copy(
            part_v.at[block(t, ch)], recv[ch].at[slot], p_ss.at[ch, t], p_rs.at[ch, slot],
            device_id=(t, my_hid), device_id_type=MESH)

    def pick_copy(t, slot, ch):
        return pltpu.make_async_remote_copy(
            picked.at[t, local_rows(ch)], theta0.at[block(slot, ch)], q_ss.at[ch, t], q_rs.at[ch, slot],
            device_id=(t, my_hid), device_id_type=MESH)

    for k in offsets:
        anc_copy(wrap(me + k, groups), me).start()
    part_load.wait()
    for ch in range(chunks):
        for s in range(groups - 1):
            part_copy(target(s), me, ch).start()

    data_t[...] = jnp.transpose(data_ref[...].astype(jnp.float32)).astype(jnp.bfloat16)
    tgt[...] = jnp.zeros_like(tgt)
    tgt[:, 0:data_rows] = tgt_ref[...]
    tails[me] = part_v[depth:depth + 2].astype(jnp.float32)
    for k in offsets:
        tail_copy(wrap(me + k, groups), me).start()
    for ch in range(chunks):
        recv[ch][me] = part_v[block(me, ch)]
    noise_copy.wait()

    for k in offsets:
        s = wrap(me + groups - k, groups)
        anc_copy(s, s).wait_recv()
    scalars = pltpu.make_async_copy(anc_all, anc_s, loc.at[2])
    scalars.start()
    scalars.wait()

    shrink = groups / (groups + 5.0)
    floor_term = 0.001 * 5.0 / (groups + 5.0)

    def finish(total, square):
        mean = total / groups
        return (shrink * (square / groups - mean * mean) + floor_term).astype(jnp.bfloat16)

    for k in offsets:
        s = wrap(me + groups - k, groups)
        tail_copy(s, s).wait_recv()

    def add_tail(i, carry):
        total, square = carry
        wide = tails[anc_s[i, 0, 0]]
        return total + wide, square + wide * wide

    zero = jnp.zeros((2, width), jnp.float32)
    tinv[0:2] = finish(*lax.fori_loop(0, groups, add_tail, (zero, zero))).astype(jnp.float32)
    tpos0[0:2] = tails[anc_s[me, 0, 0]]
    tpos[0:2] = tpos0[0:2]
    tmom[0:2] = noise_v[depth:depth + 2].astype(jnp.float32) * lax.rsqrt(tinv[0:2])

    place, inner = me // 2, lax.rem(me, 2)

    def mass_copy(t, who, ch, sem):
        return pltpu.make_async_remote_copy(
            mass.at[block(who, ch)], mass.at[block(who, ch)], sem.at[ch, who], mass_rs.at[ch, who],
            device_id=(t, my_hid), device_id_type=MESH)

    def spread(who, ch, up, down):
        @pl.when(lax.rem(my_hid, 2) == 1)
        def _():
            mass_copy(me + 1 - 2 * inner, who, ch, side_ss).start()

        if up:
            @pl.when(place < half - 1)
            def _():
                mass_copy(me + 2, who, ch, up_ss).start()
        if down:
            @pl.when(place > 0)
            def _():
                mass_copy(me - 2, who, ch, down_ss).start()

        @pl.when(lax.rem(my_hid, 2) == 0)
        def _():
            mass_copy(me + 1 - 2 * inner, who, ch, side_ss).start()

    inward = 1 - 2 * (place // 2)
    is_end = (place == 0) | (place == half - 1)
    step = 2 * inward
    partner = me + 1 - 2 * inner

    def send_own(ch):
        if half != 4:
            spread(me, ch, True, True)
            return

        @pl.when(is_end)
        def _():
            mass_copy(me + step, me, ch, up_ss).start()
            mass_copy(me + 2 * step, me, ch, down_ss).start()

        @pl.when(jnp.logical_not(is_end))
        def _():
            mass_copy(me + step, me, ch, up_ss).start()
            mass_copy(me - step, me, ch, down_ss).start()

        mass_copy(partner, me, ch, side_ss).start()

    def relay(s, ch):
        @pl.when(is_end)
        def _():
            if s == 1:
                mass_copy(me, partner, ch, up_ss).wait_recv()
                mass_copy(me + step, partner, ch, up_ss).start()
            for far_off in ((), (1,), (2, 3))[s - 1]:
                who = me + far_off * step
                mass_copy(me, who, ch, up_ss).wait_recv()
                mass_copy(partner, who, ch, side_ss).start()

        @pl.when(jnp.logical_not(is_end))
        def _():
            if s < 3:
                who = me + s * step
                mass_copy(me, who, ch, up_ss).wait_recv()
                mass_copy(me - step, who, ch, down_ss).start()
                mass_copy(partner, who, ch, side_ss).start()

    def rest_of_mass(ch):
        if half != 4:
            for q in range(half):
                mass_copy(me, 2 * q + 1 - inner, ch, side_ss).wait_recv()
            return

        @pl.when(is_end)
        def _():
            for far_off in (1, 2, 3):
                mass_copy(me, partner + far_off * step, ch, side_ss).wait_recv()

        @pl.when(jnp.logical_not(is_end))
        def _():
            mass_copy(me, me - step, ch, side_ss).wait_recv()
            mass_copy(me, partner - step, ch, side_ss).wait_recv()
            for far_off in (0, 1, 2):
                mass_copy(me, partner + far_off * step, ch, side_ss).wait_recv()

    def mass_sent(ch):
        if half != 4:
            for q in range(half):
                who = 2 * q + inner
                mass_copy(me, who, ch, side_ss).wait_send()

                @pl.when((q <= place) & (place < half - 1))
                def _():
                    mass_copy(me, who, ch, up_ss).wait_send()

                @pl.when((q >= place) & (place > 0))
                def _():
                    mass_copy(me, who, ch, down_ss).wait_send()
            return
        mass_copy(me, me, ch, up_ss).wait_send()
        mass_copy(me, me, ch, down_ss).wait_send()
        mass_copy(me, me, ch, side_ss).wait_send()

        @pl.when(is_end)
        def _():
            mass_copy(me, partner, ch, up_ss).wait_send()
            for far_off in (1, 2, 3):
                mass_copy(me, me + far_off * step, ch, side_ss).wait_send()

        @pl.when(jnp.logical_not(is_end))
        def _():
            for far_off in (1, 2):
                mass_copy(me, me + far_off * step, ch, side_ss).wait_send()
                mass_copy(me, me + far_off * step, ch, down_ss).wait_send()

    def select(ch):
        for k in offsets:
            s = wrap(me + groups - k, groups)
            part_copy(s, s, ch).wait_recv()

        @pl.loop(0, piece // CHUNK)
        def _(r):
            here = pl.ds(pl.multiple_of(ch * piece + r * CHUNK, CHUNK), CHUNK)

            def add(i, carry):
                total, square = carry
                got = recv[ch][anc_s[i, 0, 0], pl.ds(pl.multiple_of(r * CHUNK, CHUNK), CHUNK)]
                picked[i, here] = got
                wide = got.astype(jnp.float32)
                return total + wide, square + wide * wide

            zero = jnp.zeros((CHUNK, width), jnp.float32)
            carry = (zero, zero)
            if groups <= 8:
                for i in range(groups):
                    carry = add(i, carry)
            else:
                carry = lax.fori_loop(0, groups, add, carry)
            there = pl.ds(pl.multiple_of(me * rows + ch * piece + r * CHUNK, CHUNK), CHUNK)
            mass[there] = finish(*carry)
            theta0[there] = picked[me, here]

    def forward_mass(s, ch):
        if half == 4:
            relay(s, ch)
            return

        @pl.when(place >= s)
        def _():
            mass_copy(me, me - 2 * s, ch, up_ss).wait_recv()
            spread(me - 2 * s, ch, True, False)

        @pl.when(place + s < half)
        def _():
            mass_copy(me, me + 2 * s, ch, up_ss).wait_recv()
            spread(me + 2 * s, ch, False, True)

    def send_picks(some):
        for s, ch in some:
            pick_copy(target(s), me, ch).start()

    last_chunk = chunks - 1
    pending = []
    for ch in range(last_chunk):
        select(ch)
        send_own(ch)
        pending += [(s, ch) for s in range(groups - 1)]
        send_picks(pending[:3])
        pending = pending[3:]
    select(last_chunk)
    pending += [(s, last_chunk) for s in range(groups - 1)]
    hops = [(s, ch) for s in range(1, half) for ch in range(last_chunk)]
    quota = -(-len(pending) // (len(hops) + 1))
    for s, ch in hops:
        send_picks(pending[:quota])
        pending = pending[quota:]
        forward_mass(s, ch)
    send_picks(pending)
    send_own(last_chunk)

    for ch in range(chunks):
        for k in offsets:
            s = wrap(me + groups - k, groups)
            pick_copy(s, s, ch).wait_recv()

    def forward(weights, cols, keep_hidden):
        pre = jnp.dot(data_ref[...], weights, preferred_element_type=jnp.float32)
        h = jnp.tanh(pre * in_scale + tpos[0:1, cols])
        if keep_hidden:
            hid[:, cols] = h
        weighted = h * tpos[1:2, cols]
        total = weighted[:, 0:128]
        for c in range(128, TILE, 128):
            total = total + weighted[:, c:c + 128]
        return total

    def tile(c):
        return pl.ds(pl.multiple_of(c * TILE, TILE), TILE)

    none = jnp.zeros((data_rows, 128), jnp.float32)
    tiles = width // TILE

    def outputs(stage, total):
        total = jnp.concatenate([total, jnp.zeros((padded - data_rows, 128), jnp.float32)], axis=0)
        flat = jnp.sum(jnp.transpose(total), axis=0, keepdims=True) * out_scale
        part_buf[stage] = jnp.broadcast_to(flat, (8, padded))

        def copy(t, slot):
            return pltpu.make_async_remote_copy(
                part_buf.at[stage], part_all.at[stage, slot], h_ss.at[stage, t], h_rs.at[stage, slot],
                device_id=(me, t), device_id_type=MESH)

        for k in range(1, hids):
            copy(wrap(my_hid + k, hids), my_hid).start()
        part_all[stage, my_hid] = part_buf[stage]
        for k in range(1, hids):
            s = wrap(my_hid + k, hids)
            copy(s, s).wait_recv()
        for k in range(1, hids):
            copy(wrap(my_hid + k, hids), my_hid).wait_send()
        result = part_all[stage, 0]
        for j in range(1, hids):
            result = result + part_all[stage, j]
        return result[0:1]

    def set_resid(result):
        r = TEMPER_LEVEL * NOISE_INV_VARIANCE * (result - tgt[...])
        column = jnp.transpose(jnp.broadcast_to(r, (128, padded)))[0:data_rows]
        for c in range(0, TILE, 128):
            resid[:, c:c + 128] = column

    keep = acc_ref[0] == 1

    def backward(cols, step):
        h = hid[:, cols]
        b, v = tpos[0:1, cols], tpos[1:2, cols]
        res = resid[...]
        grad_v = jnp.sum(res * h, axis=0, keepdims=True) * out_scale + v
        back = res * (v * out_scale) * (1.0 - h * h)
        grad_b = jnp.sum(back, axis=0, keepdims=True) + b
        grad = jnp.dot(data_t[...], back.astype(jnp.bfloat16), preferred_element_type=jnp.float32) * in_scale
        tm = tmom[0:2, cols] - step * jnp.concatenate([grad_b, grad_v], axis=0)
        tmom[0:2, cols] = tm
        tpos[0:2, cols] = tpos[0:2, cols] + STEP_SIZE * tinv[0:2, cols] * tm
        return grad

    start = lax.fori_loop(
        0, tiles, lambda c, total: total + forward(theta0[:, tile(c)], tile(c), True), none)
    outputs0 = outputs(0, start)
    set_resid(outputs0)
    forward_mass(1, last_chunk)

    @pl.loop(0, tiles)
    def _(c):
        cols = tile(c)
        mom[:, cols] = backward(cols, 0.5 * STEP_SIZE) + theta0[:, cols].astype(jnp.float32)

    for s in range(2, half):
        forward_mass(s, last_chunk)
    for ch in range(chunks):
        rest_of_mass(ch)

    def first_move(c, total):
        cols = tile(c)
        inv = mass[:, cols].astype(jnp.float32)
        m = noise_v[0:depth, cols].astype(jnp.float32) * lax.rsqrt(inv) - 0.5 * STEP_SIZE * mom[:, cols]
        w = theta0[:, cols].astype(jnp.float32) + STEP_SIZE * inv * m
        mom[:, cols] = m
        pos[:, cols] = w
        return total + forward(w.astype(jnp.bfloat16), cols, True)

    def last_move(c, total):
        cols = tile(c)
        w = pos[:, cols]
        m = mom[:, cols] - STEP_SIZE * (backward(cols, STEP_SIZE) + w)
        w = w + STEP_SIZE * mass[:, cols].astype(jnp.float32) * m
        moved[0:depth, cols] = jnp.where(keep, w, theta0[:, cols].astype(jnp.float32)).astype(jnp.bfloat16)
        return total + forward(w.astype(jnp.bfloat16), cols, False)

    set_resid(outputs(1, lax.fori_loop(0, tiles, first_move, none)))
    last = lax.fori_loop(0, tiles, last_move, none)
    moved[depth:depth + 2] = jnp.where(keep, tpos[0:2], tpos0[0:2]).astype(jnp.bfloat16)
    result_copy = pltpu.make_async_copy(moved, main_out.at[0], loc.at[3])
    result_copy.start()
    outputs2 = outputs(2, last)
    miss = tgt[...] - jnp.where(keep, outputs2, outputs0)
    fit_out[...] = jnp.broadcast_to(jnp.sum(miss * miss, axis=1, keepdims=True) / data_rows, fit_out.shape)

    result_copy.wait()
    for k in offsets:
        t = wrap(me + k, groups)
        anc_copy(t, me).wait_send()
        tail_copy(t, me).wait_send()
    for ch in range(chunks):
        for k in offsets:
            t = wrap(me + k, groups)
            part_copy(t, me, ch).wait_send()
            pick_copy(t, me, ch).wait_send()
        mass_sent(ch)


def body(groups, hids, particles, noise, ancestors, accepted, data, targets):
    _, rows_all, width = particles.shape
    depth = rows_all - 2
    rows = depth // groups
    chunks = min(CHUNKS, rows // CHUNK)
    data_rows = data.shape[0]
    padded = -(-data_rows // 128) * 128
    bf, f32 = jnp.bfloat16, jnp.float32
    vm = pl.BlockSpec(memory_space=pltpu.VMEM)
    sm = pl.BlockSpec(memory_space=pltpu.SMEM)
    anywhere = pl.BlockSpec(memory_space=pl.ANY)
    dma = pltpu.SemaphoreType.DMA
    moved, fit = pl.pallas_call(
        functools.partial(kernel, groups, hids, chunks),
        out_shape=(
            jax.ShapeDtypeStruct((1, rows_all, width), bf),
            jax.ShapeDtypeStruct((1, 128), f32),
        ),
        in_specs=[sm, sm, anywhere, anywhere, vm, vm],
        out_specs=(anywhere, vm),
        scratch_shapes=[
            pltpu.VMEM((groups, 1, 128), jnp.int32),
            pltpu.SMEM((groups, 1, 128), jnp.int32),
            pltpu.VMEM((groups, 2, width), f32),
            [pltpu.VMEM((groups, rows // chunks, width), bf)] * chunks,
            pltpu.VMEM((groups, rows, width), bf),
            pltpu.VMEM((depth, width), bf),
            pltpu.VMEM((depth, width), bf),
            pltpu.VMEM((rows_all, width), bf),
            pltpu.VMEM((rows_all, width), bf),
            pltpu.VMEM((depth, data_rows), bf),
            pltpu.VMEM((depth, width), f32),
            pltpu.VMEM((depth, width), f32),
            pltpu.VMEM((rows_all, width), bf),
            pltpu.VMEM((data_rows, width), f32),
            pltpu.VMEM((data_rows, TILE), f32),
            pltpu.VMEM((1, padded), f32),
            pltpu.VMEM((8, width), f32),
            pltpu.VMEM((8, width), f32),
            pltpu.VMEM((8, width), f32),
            pltpu.VMEM((8, width), f32),
            pltpu.VMEM((3, 8, padded), f32),
            pltpu.VMEM((3, hids, 8, padded), f32),
        ] + [dma((groups,))] * 4 + [dma((chunks, groups))] * 8 + [dma((3, hids))] * 2 + [dma((4,))],
        compiler_params=pltpu.CompilerParams(
            collective_id=0, has_side_effects=True, vmem_limit_bytes=56 * 1024 * 1024),
        cost_estimate=pl.CostEstimate(
            flops=10 * data_rows * depth * width, bytes_accessed=8 * depth * width,
            transcendentals=3 * data_rows * width),
    )(ancestors, accepted, particles, noise, data, targets[None])
    return moved, fit[0, :1]


def solution(mesh):
    groups, hids = mesh.shape["dom"], mesh.shape["hid"]
    return jax.shard_map(
        functools.partial(body, groups, hids),
        mesh=mesh,
        in_specs=(P("dom", None, "hid"), P("dom", None, "hid"), P("dom"), P("dom"), P(), P()),
        out_specs=(P("dom", None, "hid"), P("dom")),
        check_vma=False,
    )
```

```python
import functools

import jax
import jax.numpy as jnp
from jax import lax
from jax.experimental import pallas as pl
from jax.experimental.pallas import tpu as pltpu
from jax.sharding import PartitionSpec as P

TEMPER_LEVEL = 0.125
NOISE_INV_VARIANCE = 4.0
STEP_SIZE = 0.4
MESH = pl.DeviceIdType.MESH
TILE = 256
CHUNK = 16
CHUNKS = 2


def kernel(
    groups, hids, chunks,
    anc_ref, acc_ref, part_ref, noise_ref, data_ref, tgt_ref,
    main_out, fit_out,
    anc_all, anc_s, tails, recv, picked, theta0, mass, part_v, noise_v, data_t, mom, pos, moved, hid, resid,
    tgt, tpos, tpos0, tmom, tinv, part_buf, part_all,
    anc_ss, anc_rs, tail_ss, tail_rs, p_ss, p_rs, q_ss, q_rs,
    up_ss, down_ss, side_ss, mass_rs, h_ss, h_rs, loc,
):
    me = lax.axis_index("dom")
    my_hid = lax.axis_index("hid")
    depth, width = theta0.shape
    rows = depth // groups
    piece = rows // chunks
    data_rows = data_ref.shape[0]
    padded = part_buf.shape[-1]
    in_scale = depth ** (-0.5)
    out_scale = (width * hids) ** (-0.5)
    half = groups // 2
    offsets = range(1, groups)
    far, near = list(range(half, groups)), list(range(1, half))
    far_first = [m for pair in zip(far, near) for m in pair] + far[half - 1:]
    near_first = [m for pair in zip(near, far) for m in pair] + far[half - 1:]

    def flip(m):
        t = me
        for bit in range(groups.bit_length() - 1):
            if m >> bit & 1:
                t = t + (1 << bit) - 2 * (1 << bit) * lax.rem(me // (1 << bit), 2)
        return t

    def target(s):
        odd = lax.rem(me // 2 + my_hid, 2)
        first, second = flip(far_first[s]), flip(near_first[s])
        return first + odd * (second - first)

    def wrap(i, n):
        return lax.rem(i, n)

    def block(i, ch):
        return pl.ds(pl.multiple_of(i * rows + ch * piece, piece), piece)

    part_load = pltpu.make_async_copy(part_ref.at[0], part_v, loc.at[1])
    part_load.start()
    noise_copy = pltpu.make_async_copy(noise_ref.at[0], noise_v, loc.at[0])
    noise_copy.start()
    anc_all[me] = jnp.full((1, 128), anc_ref[0], jnp.int32)

    barrier = pltpu.get_barrier_semaphore()
    for k in range(1, groups):
        pl.semaphore_signal(barrier, inc=1, device_id=(wrap(me + k, groups), my_hid), device_id_type=MESH)
    for k in range(1, hids):
        pl.semaphore_signal(barrier, inc=1, device_id=(me, wrap(my_hid + k, hids)), device_id_type=MESH)
    pl.semaphore_wait(barrier, groups - 1 + hids - 1)

    def anc_copy(t, slot):
        return pltpu.make_async_remote_copy(
            anc_all.at[slot], anc_all.at[slot], anc_ss.at[t], anc_rs.at[slot],
            device_id=(t, my_hid), device_id_type=MESH)

    def tail_copy(t, slot):
        return pltpu.make_async_remote_copy(
            tails.at[slot], tails.at[slot], tail_ss.at[t], tail_rs.at[slot],
            device_id=(t, my_hid), device_id_type=MESH)

    def local_rows(ch):
        return pl.ds(ch * piece, piece)

    def part_copy(t, slot, ch):
        return pltpu.make_async_remote_copy(
            part_v.at[block(t, ch)], recv[ch].at[slot], p_ss.at[ch, t], p_rs.at[ch, slot],
            device_id=(t, my_hid), device_id_type=MESH)

    def pick_copy(t, slot, ch):
        return pltpu.make_async_remote_copy(
            picked.at[t, local_rows(ch)], theta0.at[block(slot, ch)], q_ss.at[ch, t], q_rs.at[ch, slot],
            device_id=(t, my_hid), device_id_type=MESH)

    for k in offsets:
        anc_copy(wrap(me + k, groups), me).start()
    part_load.wait()
    for ch in range(chunks):
        for s in range(groups - 1):
            part_copy(target(s), me, ch).start()

    data_t[...] = jnp.transpose(data_ref[...].astype(jnp.float32)).astype(jnp.bfloat16)
    tgt[...] = jnp.zeros_like(tgt)
    tgt[:, 0:data_rows] = tgt_ref[...]
    tails[me] = part_v[depth:depth + 2].astype(jnp.float32)
    for k in offsets:
        tail_copy(wrap(me + k, groups), me).start()
    for ch in range(chunks):
        recv[ch][me] = part_v[block(me, ch)]
    noise_copy.wait()

    for k in offsets:
        s = wrap(me + groups - k, groups)
        anc_copy(s, s).wait_recv()
    scalars = pltpu.make_async_copy(anc_all, anc_s, loc.at[2])
    scalars.start()
    scalars.wait()

    shrink = groups / (groups + 5.0)
    floor_term = 0.001 * 5.0 / (groups + 5.0)

    def finish(total, square):
        mean = total / groups
        return (shrink * (square / groups - mean * mean) + floor_term).astype(jnp.bfloat16)

    for k in offsets:
        s = wrap(me + groups - k, groups)
        tail_copy(s, s).wait_recv()

    def add_tail(i, carry):
        total, square = carry
        wide = tails[anc_s[i, 0, 0]]
        return total + wide, square + wide * wide

    zero = jnp.zeros((2, width), jnp.float32)
    tinv[0:2] = finish(*lax.fori_loop(0, groups, add_tail, (zero, zero))).astype(jnp.float32)
    tpos0[0:2] = tails[anc_s[me, 0, 0]]
    tpos[0:2] = tpos0[0:2]
    tmom[0:2] = noise_v[depth:depth + 2].astype(jnp.float32) * lax.rsqrt(tinv[0:2])

    place, inner = me // 2, lax.rem(me, 2)

    def mass_copy(t, who, ch, sem):
        return pltpu.make_async_remote_copy(
            mass.at[block(who, ch)], mass.at[block(who, ch)], sem.at[ch, who], mass_rs.at[ch, who],
            device_id=(t, my_hid), device_id_type=MESH)

    def spread(who, ch, up, down):
        @pl.when(lax.rem(my_hid, 2) == 1)
        def _():
            mass_copy(me + 1 - 2 * inner, who, ch, side_ss).start()

        if up:
            @pl.when(place < half - 1)
            def _():
                mass_copy(me + 2, who, ch, up_ss).start()
        if down:
            @pl.when(place > 0)
            def _():
                mass_copy(me - 2, who, ch, down_ss).start()

        @pl.when(lax.rem(my_hid, 2) == 0)
        def _():
            mass_copy(me + 1 - 2 * inner, who, ch, side_ss).start()

    inward = 1 - 2 * (place // 2)
    is_end = (place == 0) | (place == half - 1)
    step = 2 * inward
    partner = me + 1 - 2 * inner

    def send_own(ch):
        if half != 4:
            spread(me, ch, True, True)
            return

        @pl.when(is_end)
        def _():
            mass_copy(me + step, me, ch, up_ss).start()
            mass_copy(me + 2 * step, me, ch, down_ss).start()

        @pl.when(jnp.logical_not(is_end))
        def _():
            mass_copy(me + step, me, ch, up_ss).start()
            mass_copy(me - step, me, ch, down_ss).start()

        mass_copy(partner, me, ch, side_ss).start()

    def relay(s, ch):
        @pl.when(is_end)
        def _():
            if s == 1:
                mass_copy(me, partner, ch, up_ss).wait_recv()
                mass_copy(me + step, partner, ch, up_ss).start()
            for far_off in ((), (1,), (2, 3))[s - 1]:
                who = me + far_off * step
                mass_copy(me, who, ch, up_ss).wait_recv()
                mass_copy(partner, who, ch, side_ss).start()

        @pl.when(jnp.logical_not(is_end))
        def _():
            if s < 3:
                who = me + s * step
                mass_copy(me, who, ch, up_ss).wait_recv()
                mass_copy(me - step, who, ch, down_ss).start()
                mass_copy(partner, who, ch, side_ss).start()

    def rest_of_mass(ch):
        if half != 4:
            for q in range(half):
                mass_copy(me, 2 * q + 1 - inner, ch, side_ss).wait_recv()
            return

        @pl.when(is_end)
        def _():
            for far_off in (1, 2, 3):
                mass_copy(me, partner + far_off * step, ch, side_ss).wait_recv()

        @pl.when(jnp.logical_not(is_end))
        def _():
            mass_copy(me, me - step, ch, side_ss).wait_recv()
            mass_copy(me, partner - step, ch, side_ss).wait_recv()
            for far_off in (0, 1, 2):
                mass_copy(me, partner + far_off * step, ch, side_ss).wait_recv()

    def mass_sent(ch):
        if half != 4:
            for q in range(half):
                who = 2 * q + inner
                mass_copy(me, who, ch, side_ss).wait_send()

                @pl.when((q <= place) & (place < half - 1))
                def _():
                    mass_copy(me, who, ch, up_ss).wait_send()

                @pl.when((q >= place) & (place > 0))
                def _():
                    mass_copy(me, who, ch, down_ss).wait_send()
            return
        mass_copy(me, me, ch, up_ss).wait_send()
        mass_copy(me, me, ch, down_ss).wait_send()
        mass_copy(me, me, ch, side_ss).wait_send()

        @pl.when(is_end)
        def _():
            mass_copy(me, partner, ch, up_ss).wait_send()
            for far_off in (1, 2, 3):
                mass_copy(me, me + far_off * step, ch, side_ss).wait_send()

        @pl.when(jnp.logical_not(is_end))
        def _():
            for far_off in (1, 2):
                mass_copy(me, me + far_off * step, ch, side_ss).wait_send()
                mass_copy(me, me + far_off * step, ch, down_ss).wait_send()

    def select(ch):
        for k in offsets:
            s = wrap(me + groups - k, groups)
            part_copy(s, s, ch).wait_recv()

        @pl.loop(0, piece // CHUNK)
        def _(r):
            here = pl.ds(pl.multiple_of(ch * piece + r * CHUNK, CHUNK), CHUNK)

            def add(i, carry):
                total, square = carry
                got = recv[ch][anc_s[i, 0, 0], pl.ds(pl.multiple_of(r * CHUNK, CHUNK), CHUNK)]
                picked[i, here] = got
                wide = got.astype(jnp.float32)
                return total + wide, square + wide * wide

            zero = jnp.zeros((CHUNK, width), jnp.float32)
            carry = (zero, zero)
            if groups <= 8:
                for i in range(groups):
                    carry = add(i, carry)
            else:
                carry = lax.fori_loop(0, groups, add, carry)
            there = pl.ds(pl.multiple_of(me * rows + ch * piece + r * CHUNK, CHUNK), CHUNK)
            mass[there] = finish(*carry)
            theta0[there] = picked[me, here]

        send_own(ch)

    def forward_mass(s, ch):
        if half == 4:
            relay(s, ch)
            return

        @pl.when(place >= s)
        def _():
            mass_copy(me, me - 2 * s, ch, up_ss).wait_recv()
            spread(me - 2 * s, ch, True, False)

        @pl.when(place + s < half)
        def _():
            mass_copy(me, me + 2 * s, ch, up_ss).wait_recv()
            spread(me + 2 * s, ch, False, True)

    stages = chunks + half - 1
    pending = []
    quota = -(-chunks * (groups - 1) // stages)
    for stage in range(stages):
        if stage < chunks:
            select(stage)
            pending += [(s, stage) for s in range(groups - 1)]
        for s, ch in pending[:quota]:
            pick_copy(target(s), me, ch).start()
        pending = pending[quota:]
        for s in range(1, half):
            if 0 <= stage - s < chunks:
                forward_mass(s, stage - s)

    for ch in range(chunks):
        for k in offsets:
            s = wrap(me + groups - k, groups)
            pick_copy(s, s, ch).wait_recv()

    def forward(weights, cols, keep_hidden):
        pre = jnp.dot(data_ref[...], weights, preferred_element_type=jnp.float32)
        h = jnp.tanh(pre * in_scale + tpos[0:1, cols])
        if keep_hidden:
            hid[:, cols] = h
        weighted = h * tpos[1:2, cols]
        total = weighted[:, 0:128]
        for c in range(128, TILE, 128):
            total = total + weighted[:, c:c + 128]
        return total

    def tile(c):
        return pl.ds(pl.multiple_of(c * TILE, TILE), TILE)

    none = jnp.zeros((data_rows, 128), jnp.float32)
    tiles = width // TILE

    def outputs(stage, total):
        total = jnp.concatenate([total, jnp.zeros((padded - data_rows, 128), jnp.float32)], axis=0)
        flat = jnp.sum(jnp.transpose(total), axis=0, keepdims=True) * out_scale
        part_buf[stage] = jnp.broadcast_to(flat, (8, padded))

        def copy(t, slot):
            return pltpu.make_async_remote_copy(
                part_buf.at[stage], part_all.at[stage, slot], h_ss.at[stage, t], h_rs.at[stage, slot],
                device_id=(me, t), device_id_type=MESH)

        for k in range(1, hids):
            copy(wrap(my_hid + k, hids), my_hid).start()
        part_all[stage, my_hid] = part_buf[stage]
        for k in range(1, hids):
            s = wrap(my_hid + k, hids)
            copy(s, s).wait_recv()
        for k in range(1, hids):
            copy(wrap(my_hid + k, hids), my_hid).wait_send()
        result = part_all[stage, 0]
        for j in range(1, hids):
            result = result + part_all[stage, j]
        return result[0:1]

    def set_resid(result):
        r = TEMPER_LEVEL * NOISE_INV_VARIANCE * (result - tgt[...])
        column = jnp.transpose(jnp.broadcast_to(r, (128, padded)))[0:data_rows]
        for c in range(0, TILE, 128):
            resid[:, c:c + 128] = column

    keep = acc_ref[0] == 1

    def backward(cols, step):
        h = hid[:, cols]
        b, v = tpos[0:1, cols], tpos[1:2, cols]
        res = resid[...]
        grad_v = jnp.sum(res * h, axis=0, keepdims=True) * out_scale + v
        back = res * (v * out_scale) * (1.0 - h * h)
        grad_b = jnp.sum(back, axis=0, keepdims=True) + b
        grad = jnp.dot(data_t[...], back.astype(jnp.bfloat16), preferred_element_type=jnp.float32) * in_scale
        tm = tmom[0:2, cols] - step * jnp.concatenate([grad_b, grad_v], axis=0)
        tmom[0:2, cols] = tm
        tpos[0:2, cols] = tpos[0:2, cols] + STEP_SIZE * tinv[0:2, cols] * tm
        return grad

    start = lax.fori_loop(
        0, tiles, lambda c, total: total + forward(theta0[:, tile(c)], tile(c), True), none)
    outputs0 = outputs(0, start)
    set_resid(outputs0)

    @pl.loop(0, tiles)
    def _(c):
        cols = tile(c)
        mom[:, cols] = backward(cols, 0.5 * STEP_SIZE) + theta0[:, cols].astype(jnp.float32)

    for ch in range(chunks):
        rest_of_mass(ch)

    def first_move(c, total):
        cols = tile(c)
        inv = mass[:, cols].astype(jnp.float32)
        m = noise_v[0:depth, cols].astype(jnp.float32) * lax.rsqrt(inv) - 0.5 * STEP_SIZE * mom[:, cols]
        w = theta0[:, cols].astype(jnp.float32) + STEP_SIZE * inv * m
        mom[:, cols] = m
        pos[:, cols] = w
        return total + forward(w.astype(jnp.bfloat16), cols, True)

    def last_move(c, total):
        cols = tile(c)
        w = pos[:, cols]
        m = mom[:, cols] - STEP_SIZE * (backward(cols, STEP_SIZE) + w)
        w = w + STEP_SIZE * mass[:, cols].astype(jnp.float32) * m
        moved[0:depth, cols] = jnp.where(keep, w, theta0[:, cols].astype(jnp.float32)).astype(jnp.bfloat16)
        return total + forward(w.astype(jnp.bfloat16), cols, False)

    set_resid(outputs(1, lax.fori_loop(0, tiles, first_move, none)))
    last = lax.fori_loop(0, tiles, last_move, none)
    moved[depth:depth + 2] = jnp.where(keep, tpos[0:2], tpos0[0:2]).astype(jnp.bfloat16)
    result_copy = pltpu.make_async_copy(moved, main_out.at[0], loc.at[3])
    result_copy.start()
    outputs2 = outputs(2, last)
    miss = tgt[...] - jnp.where(keep, outputs2, outputs0)
    fit_out[...] = jnp.broadcast_to(jnp.sum(miss * miss, axis=1, keepdims=True) / data_rows, fit_out.shape)

    result_copy.wait()
    for k in offsets:
        t = wrap(me + k, groups)
        anc_copy(t, me).wait_send()
        tail_copy(t, me).wait_send()
    for ch in range(chunks):
        for k in offsets:
            t = wrap(me + k, groups)
            part_copy(t, me, ch).wait_send()
            pick_copy(t, me, ch).wait_send()
        mass_sent(ch)


def body(groups, hids, particles, noise, ancestors, accepted, data, targets):
    _, rows_all, width = particles.shape
    depth = rows_all - 2
    rows = depth // groups
    chunks = min(CHUNKS, rows // CHUNK)
    data_rows = data.shape[0]
    padded = -(-data_rows // 128) * 128
    bf, f32 = jnp.bfloat16, jnp.float32
    vm = pl.BlockSpec(memory_space=pltpu.VMEM)
    sm = pl.BlockSpec(memory_space=pltpu.SMEM)
    anywhere = pl.BlockSpec(memory_space=pl.ANY)
    dma = pltpu.SemaphoreType.DMA
    moved, fit = pl.pallas_call(
        functools.partial(kernel, groups, hids, chunks),
        out_shape=(
            jax.ShapeDtypeStruct((1, rows_all, width), bf),
            jax.ShapeDtypeStruct((1, 128), f32),
        ),
        in_specs=[sm, sm, anywhere, anywhere, vm, vm],
        out_specs=(anywhere, vm),
        scratch_shapes=[
            pltpu.VMEM((groups, 1, 128), jnp.int32),
            pltpu.SMEM((groups, 1, 128), jnp.int32),
            pltpu.VMEM((groups, 2, width), f32),
            [pltpu.VMEM((groups, rows // chunks, width), bf)] * chunks,
            pltpu.VMEM((groups, rows, width), bf),
            pltpu.VMEM((depth, width), bf),
            pltpu.VMEM((depth, width), bf),
            pltpu.VMEM((rows_all, width), bf),
            pltpu.VMEM((rows_all, width), bf),
            pltpu.VMEM((depth, data_rows), bf),
            pltpu.VMEM((depth, width), f32),
            pltpu.VMEM((depth, width), f32),
            pltpu.VMEM((rows_all, width), bf),
            pltpu.VMEM((data_rows, width), f32),
            pltpu.VMEM((data_rows, TILE), f32),
            pltpu.VMEM((1, padded), f32),
            pltpu.VMEM((8, width), f32),
            pltpu.VMEM((8, width), f32),
            pltpu.VMEM((8, width), f32),
            pltpu.VMEM((8, width), f32),
            pltpu.VMEM((3, 8, padded), f32),
            pltpu.VMEM((3, hids, 8, padded), f32),
        ] + [dma((groups,))] * 4 + [dma((chunks, groups))] * 8 + [dma((3, hids))] * 2 + [dma((4,))],
        compiler_params=pltpu.CompilerParams(
            collective_id=0, has_side_effects=True, vmem_limit_bytes=56 * 1024 * 1024),
        cost_estimate=pl.CostEstimate(
            flops=10 * data_rows * depth * width, bytes_accessed=8 * depth * width,
            transcendentals=3 * data_rows * width),
    )(ancestors, accepted, particles, noise, data, targets[None])
    return moved, fit[0, :1]


def solution(mesh):
    groups, hids = mesh.shape["dom"], mesh.shape["hid"]
    return jax.shard_map(
        functools.partial(body, groups, hids),
        mesh=mesh,
        in_specs=(P("dom", None, "hid"), P("dom", None, "hid"), P("dom"), P("dom"), P(), P()),
        out_specs=(P("dom", None, "hid"), P("dom")),
        check_vma=False,
    )
```
